512 devices in a mesh: dp: 64 (over x, y, core), tensor: 8 (over z).
Axes of the slice: x: 4, y: 8, z: 8, core: 2. Of those that a mesh axis runs over, the one named last changes fastest.
Arguments:
- tokens: bfloat16 [8192, 8192], P('dp', 'tensor'), may hold values from -6 to 6
- value_weight: bfloat16 [8192, 1024], P('tensor'), may hold values from -0.0625 to 0.0625
- down_panels: bfloat16 [64, 8192, 64], P('dp', 'tensor'), may hold values from -0.0625 to 0.0625
- up_panels: bfloat16 [64, 64, 1024], P('dp', None, 'tensor'), may hold values from -0.1875 to 0.1875
- output_gradient: bfloat16 [8192, 1024], P('dp', 'tensor'), may hold values from -6 to 6
- sequence_adapter: int32 [512, 1], P('dp'), may hold values from 0 to 63
- sequence_lengths: int32 [64, 8], P('dp'), may hold values from 1 to 64, 128 in all within a row
- owner_slot_table: int32 [64], replicated, may hold values from 0 to 63, each once
Outputs:
- values: bfloat16 [8192, 1024], P('dp', 'tensor')
- token_gradient: bfloat16 [8192, 8192], P('dp', 'tensor')
- grad_a: float32 [64, 8192, 64], P('dp', 'tensor')
- grad_b: float32 [64, 64, 1024], P('dp', None, 'tensor')
The draws below stay inside these ranges and needn't reach their ends.
Inputs may be any that keep to these rules, and one draw needn't show every extreme that they name: `sequence_adapter`: every adapter id is named by at least one sequence. `sequence_lengths`: each row sums to 128; some entry equals 64. `owner_slot_table`: each slot appears exactly once.
All inputs are finite; a program needn't handle non-finite values.
Results may differ from the reference program's by a relative error of at most 0.0075.
Values may be sent and summed in bfloat16 or wider, within the bound.
A program may use at most 64 MiB of HBM per device.

```python
import math
import jax
import jax.numpy as jnp
import numpy as np
from jax import lax

MODEL_WIDTH = 8192
VALUE_WIDTH = 1024
ADAPTER_RANK = 64
SEQUENCES_LOCAL = 8
TOK_DEV = 128
SEG_MOST = 64
ADAPTER_COUNT = 64
SEGS = 512
TOKENS = 8192
N_DP = 64


def steps_of(own_key, dims, shards, least, high):
    factor_of, own = 1.0, jax.random.fold_in(own_key, 6)
    for dim, parts in shards:
        heights = jnp.exp(jax.random.uniform(jax.random.fold_in(own, dim), (parts,), jnp.float32, least / len(shards), high / len(shards)))
        factor_of = factor_of * jnp.repeat(heights, dims[dim] // parts).reshape([-1 if axis == dim else 1 for axis in range(len(dims))])
    return factor_of


def different_ones(stream_key, rows, number_of, top, lift):
    sequence = jax.random.permutation(jax.random.fold_in(stream_key, 1), number_of)
    favour = sequence
    for power in range(3):
        favour = favour * favour // number_of
    favour = favour * lift // number_of
    tickets = jax.random.randint(jax.random.fold_in(stream_key, 2), (rows, number_of), 0, 4096) + favour
    fixed_rows = jax.random.permutation(jax.random.fold_in(stream_key, 3), rows)[jnp.arange(number_of) % rows]
    tickets = jnp.where(jnp.arange(rows)[:, None] == fixed_rows[None, :], 1 << 14, tickets)
    priority = tickets * number_of + jnp.arange(number_of)
    return lax.top_k(priority.astype(jnp.int32), top)[1].astype(jnp.int32)


def length_profile(amount, total, reach, lean):
    weights = [(1 << 20) // math.isqrt(rank ** lean) + 1 for rank in range(2, amount + 1)]
    surplus, given = total - reach - (amount - 1), [1] * (amount - 1)
    while surplus > 0:
        movable = [i for i in range(amount - 1) if given[i] < reach]
        pool, budget = sum([weights[i] for i in movable]), surplus
        for i in movable:
            addition = min(reach - given[i], max(1, budget * weights[i] // pool), surplus)
            given[i] = given[i] + addition
            surplus = surplus - addition
    return np.array([reach] + given)


def ragged_sizes(key, number_of, total, reach, skew):
    if number_of == 2:
        one = jax.random.randint(key, (), max(1, total - reach), min(reach, total - 1) + 1)
        return jnp.stack([one, total - one])
    tallies = jnp.asarray(length_profile(number_of, total, reach, skew), jnp.int32)
    pairs = (number_of - 1) // 2
    donor, sink = tallies[1:1 + 2 * pairs:2], tallies[2:2 + 2 * pairs:2]
    margin = jnp.minimum(donor - 1, reach - sink)
    moved = jax.random.randint(jax.random.fold_in(key, 1), (pairs,), 0, 1 << 20) % (margin + 1)
    tallies = tallies.at[1:1 + 2 * pairs:2].set(donor - moved).at[2:2 + 2 * pairs:2].set(sink + moved)
    return tallies[jax.random.permutation(jax.random.fold_in(key, 2), number_of)]


def centred(rng, dims, spread, most, split=(), kind=jnp.bfloat16):
    factor_of = steps_of(rng, dims, split, -0.22, 0.18) if split else 1.0
    entries = jax.random.normal(rng, dims, jnp.float32) * spread * factor_of
    return jnp.minimum(jnp.maximum(entries, -most), most).astype(kind)


def setup_inputs(seed: int = 0) -> dict:
    splits = jax.random.split(jax.random.key(seed), 9)
    tokens = centred(splits[0], (TOKENS, MODEL_WIDTH), 1.0, 6.0, ((0, 64), (1, 8)))
    value_weight = centred(splits[1], (MODEL_WIDTH, VALUE_WIDTH), MODEL_WIDTH ** -0.5, 0.0625, ((0, 8),))
    down_panels = centred(splits[2], (ADAPTER_COUNT, MODEL_WIDTH, ADAPTER_RANK), MODEL_WIDTH ** -0.5, 0.0625, ((0, 64), (1, 8)))
    up_panels = centred(splits[3], (ADAPTER_COUNT, ADAPTER_RANK, VALUE_WIDTH), VALUE_WIDTH ** -0.5, 0.1875, ((0, 64), (2, 8)))
    output_gradient = centred(splits[4], (TOKENS, VALUE_WIDTH), 1.0, 6.0, ((0, 64), (1, 8)))
    sequence_adapter = different_ones(splits[5], SEGS, ADAPTER_COUNT, 1, 128)
    sequence_lengths = jax.vmap(lambda own: ragged_sizes(own, SEQUENCES_LOCAL, TOK_DEV, SEG_MOST, 1))(jax.random.split(splits[6], N_DP)).reshape((N_DP, SEQUENCES_LOCAL)).astype(jnp.int32)
    owner_slot_table = jax.random.permutation(splits[7], ADAPTER_COUNT).astype(jnp.int32)
    return {"tokens": tokens, "value_weight": value_weight, "down_panels": down_panels, "up_panels": up_panels, "output_gradient": output_gradient, "sequence_adapter": sequence_adapter, "sequence_lengths": sequence_lengths, "owner_slot_table": owner_slot_table}


ADAPTER_SCALE = 2.0


def expanded_rows(narrow, sequence_mask):
    wide = narrow[:, None, :] * sequence_mask[:, :, None].astype(narrow.dtype)
    return wide.reshape(TOK_DEV, SEQUENCES_LOCAL * ADAPTER_RANK)


def grouped(wide, sequence_mask):
    return jnp.sum(wide.reshape(TOK_DEV, SEQUENCES_LOCAL, ADAPTER_RANK) * sequence_mask[:, :, None], axis=1)


def reference(tokens, value_weight, down_panels, up_panels, output_gradient, sequence_adapter, sequence_lengths, owner_slot_table):
    blocks_x = tokens.reshape(N_DP, TOK_DEV, MODEL_WIDTH)
    blocks_dy = output_gradient.reshape(N_DP, TOK_DEV, VALUE_WIDTH)
    slot_table = owner_slot_table[sequence_adapter[:, 0]].astype(jnp.int32).reshape(N_DP, SEQUENCES_LOCAL)

    def one_block(carry, inputs):
        grad_a, grad_b = carry
        block_x, block_dy, lengths, owner_slots = inputs
        seg_ends = jnp.cumsum(lengths)
        position = jnp.arange(TOK_DEV, dtype=jnp.int32)
        segment = jnp.sum((position[:, None] >= seg_ends[None, :]).astype(jnp.int32), axis=1)
        sequence_mask = (segment[:, None] == jnp.arange(SEQUENCES_LOCAL, dtype=jnp.int32)[None, :]).astype(jnp.float32)
        down_joined = jnp.transpose(down_panels[owner_slots], (1, 0, 2)).reshape(MODEL_WIDTH, SEQUENCES_LOCAL * ADAPTER_RANK)
        up_joined = up_panels[owner_slots].reshape(SEQUENCES_LOCAL * ADAPTER_RANK, VALUE_WIDTH)
        down_total = grouped(jnp.dot(block_x, down_joined, preferred_element_type=jnp.float32), sequence_mask)
        rank_activations = expanded_rows((ADAPTER_SCALE * down_total).astype(jnp.bfloat16), sequence_mask)
        block_values = (jnp.dot(block_x, value_weight, preferred_element_type=jnp.float32)
                        + jnp.dot(rank_activations, up_joined, preferred_element_type=jnp.float32)).astype(jnp.bfloat16)
        backward_total = grouped(jnp.dot(block_dy, up_joined.T, preferred_element_type=jnp.float32), sequence_mask)
        rank_gradient = expanded_rows((ADAPTER_SCALE * backward_total).astype(jnp.bfloat16), sequence_mask)
        block_grad = (jnp.dot(block_dy, value_weight.T, preferred_element_type=jnp.float32)
                      + jnp.dot(rank_gradient, down_joined.T, preferred_element_type=jnp.float32)).astype(jnp.bfloat16)
        rows_term = jnp.dot(block_x.T, rank_gradient, preferred_element_type=jnp.float32)
        rows_term = jnp.transpose(rows_term.reshape(MODEL_WIDTH, SEQUENCES_LOCAL, ADAPTER_RANK), (1, 0, 2))
        cols_term = jnp.dot(rank_activations.T, block_dy, preferred_element_type=jnp.float32).reshape(SEQUENCES_LOCAL, ADAPTER_RANK, VALUE_WIDTH)
        grad_a = grad_a.at[owner_slots].add(rows_term)
        grad_b = grad_b.at[owner_slots].add(cols_term)
        return (grad_a, grad_b), (block_values, block_grad)

    start = (jnp.zeros((ADAPTER_COUNT, MODEL_WIDTH, ADAPTER_RANK), jnp.float32), jnp.zeros((ADAPTER_COUNT, ADAPTER_RANK, VALUE_WIDTH), jnp.float32))
    (grad_a, grad_b), (values, token_gradient) = lax.scan(one_block, start, (blocks_x, blocks_dy, sequence_lengths, slot_table))
    return values.reshape(TOKENS, VALUE_WIDTH), token_gradient.reshape(TOKENS, MODEL_WIDTH), grad_a, grad_b
```

```python
import functools

import jax
import jax.numpy as jnp
from jax import lax
from jax.experimental import pallas as pl
from jax.experimental.pallas import tpu as pltpu
from jax.sharding import PartitionSpec as P

MESH = pl.DeviceIdType.MESH
BF = jnp.bfloat16
F32 = jnp.float32
NT = (((1,), (1,)), ((), ()))
T = 128
R = 64
C = 128

(S_DT, S_DY, S_SL, S_X, S_DYZ, S_U, S_LGP, S_LGZ, S_LGR, S_BZ, S_LRP, S_LRZ, S_LRR, S_TG, S_VC, S_GB, S_GA) = range(17)
N_STAGES = 17


def ring_steps(ny, d, h):
    return ny // 2 if d == h else ny - 1 - ny // 2


def kernel(
    nx, ny, nz,
    x_hbm, w_hbm, dt_hbm, u_hbm, dy_hbm, adp, lens, tab,
    v_out, tg_out, ga_out, gb_out,
    xv, wv, xr, dg, dyr, slw, slo, dyf, ug,
    lgps, lgp, lgzs, lgz, lgs, lgt,
    bs, bz, fz,
    lracc, lrps, lrp, lrzs, lrz, lrs, lrt,
    mbig, mt, two, st, tgacc, tgs, tgc, vcs, vc, pbs, gbp,
    pa, pas, rb, fin,
    ss, rs, ag_s, ag_r, rs_s, rs_r, ld,
):
    rw = 2 * nx
    hw = rw // 2
    me = lax.axis_index("dp")
    z = lax.axis_index("tensor")
    c = me % 2
    y = (me // 2) % ny
    x = me // (2 * ny)
    j = x * 2 + c

    def row_dev(jj):
        return (jj // 2) * (2 * ny) + y * 2 + jj % 2

    def y_dev(yy):
        return x * (2 * ny) + yy * 2 + c

    def slot_id(jj, yy):
        return (jj // 2) * (2 * ny) + yy * 2 + jj % 2

    def col(i):
        return pl.ds(pl.multiple_of(i * 128, 128), 128)

    def rcopy(src, dst, s, r, dev):
        return pltpu.make_async_remote_copy(
            src_ref=src, dst_ref=dst, send_sem=s, recv_sem=r, device_id=dev, device_id_type=MESH
        )

    def exchange(n, mine, dev, src, dst, stage):
        @pl.loop(1, n)
        def _(i):
            q = (mine + i) % n
            rcopy(src(q), dst, ss.at[stage], rs.at[stage], dev(q)).start()

        pltpu.make_async_copy(src(mine), dst, rs.at[stage]).start()

    def row_exchange(src, dst, stage):
        exchange(rw, j, lambda q: (row_dev(q), z), src, dst, stage)

    def y_exchange(src, dst, stage):
        exchange(ny, y, lambda q: (y_dev(q), z), src, dst, stage)

    def z_exchange(src, dst, stage):
        exchange(nz, z, lambda q: (me, q), src, dst, stage)

    def got(ref, stage):
        pltpu.make_async_copy(ref, ref, rs.at[stage]).wait()

    barrier = pltpu.get_barrier_semaphore()

    @pl.loop(1, rw)
    def _(i):
        pl.semaphore_signal(barrier, inc=1, device_id=(row_dev((j + i) % rw), z), device_id_type=MESH)

    @pl.loop(1, ny)
    def _(i):
        pl.semaphore_signal(barrier, inc=1, device_id=(y_dev((y + i) % ny), z), device_id_type=MESH)

    @pl.loop(1, nz)
    def _(i):
        pl.semaphore_signal(barrier, inc=1, device_id=(me, (z + i) % nz), device_id_type=MESH)

    load_w = pltpu.make_async_copy(w_hbm, wv, ld.at[0])
    load_x = pltpu.make_async_copy(x_hbm, xv, ld.at[1])
    load_x.start()
    load_w.start()

    position = lax.broadcasted_iota(jnp.int32, (8, T), 1)
    slots = jnp.full((8, T), 0, jnp.int32)
    begin = jnp.int32(0)
    for k in range(8):
        slots = jnp.where(position >= begin, tab[adp[k]], slots)
        begin = begin + lens[k]
    slo[...] = slots

    pl.semaphore_wait(barrier, rw + ny + nz - 3)

    y_exchange(lambda q: u_hbm, ug.at[y], S_U)
    row_exchange(lambda q: dt_hbm.at[:, col(q)], dg.at[y, j], S_DT)
    row_exchange(lambda q: slo, slw.at[:, col(j)], S_SL)
    row_exchange(lambda q: dy_hbm, dyr.at[j], S_DY)
    row_exchange(lambda q: x_hbm.at[:, col(q)], xr.at[j], S_X)
    z_exchange(lambda q: dy_hbm, dyf.at[:, col(z)], S_DYZ)

    load_x.wait()
    load_w.wait()

    @pl.loop(0, nz // 2)
    def _(i):
        part = jnp.dot(
            xv[...], wv[:, pl.ds(pl.multiple_of(i * 256, 256), 256)], preferred_element_type=F32
        ).astype(BF)
        bs[2 * i] = part[:, :C]
        bs[2 * i + 1] = part[:, C:]

    z_exchange(lambda q: bs.at[q], bz.at[z], S_BZ)

    def half(h):
        return pl.ds(h * hw, hw)

    def ag_copy(d, h, s):
        yy = (y - (s - 1) if d == 0 else y + (s - 1)) % ny
        to = (y + 1 if d == 0 else y - 1) % ny
        block = dg.at[yy, half(h)]
        return rcopy(block, block, ag_s.at[d, h, s - 1], ag_r.at[d, h, s - 1], (y_dev(to), z))

    def ag_send(s):
        for h in range(2):
            for d in range(2):
                if s <= ring_steps(ny, d, h):
                    ag_copy(d, h, s).start()

    def ag_got(s):
        for h in range(2):
            for d in range(2):
                if s <= ring_steps(ny, d, h):
                    yy = (y - s if d == 0 else y + s) % ny
                    block = dg.at[yy, half(h)]
                    pltpu.make_async_copy(block, block, ag_r.at[d, h, s - 1]).wait()
                    if s + 1 <= ring_steps(ny, d, h):
                        ag_copy(d, h, s + 1).start()

    got(dg.at[y], S_DT)
    ag_send(1)

    got(ug, S_U)
    got(slw, S_SL)
    got(dyr, S_DY)

    @pl.loop(0, rw)
    def _(b):
        wide = lax.dot_general(
            ug[...].reshape(ny * R, C), dyr[b], NT, preferred_element_type=F32
        )
        of = slw[0:1, col(b)]
        total = jnp.zeros((R, T), F32)
        for yy in range(ny):
            total = total + jnp.where(of == slot_id(j, yy), wide[yy * R : (yy + 1) * R], 0.0)
        lgps[b] = total.astype(BF)

    row_exchange(lambda q: lgps.at[q], lgp.at[j], S_LGP)

    got(dyf, S_DYZ)

    @pl.loop(0, rw // 2)
    def _(i):
        f = pl.ds(pl.multiple_of(i * 256, 256), 256)
        fz[:, f] = lax.dot_general(dyf[...], wv[f, :], NT, preferred_element_type=F32)

    def sum_of(ref, n):
        total = ref[0].astype(F32)
        for i in range(1, n):
            total = total + ref[i].astype(F32)
        return total

    got(lgp, S_LGP)
    lgzs[...] = sum_of(lgp, rw).astype(BF)
    z_exchange(lambda q: lgzs, lgz.at[z], S_LGZ)

    ag_got(1)

    got(lgz, S_LGZ)
    lgs[...] = (2.0 * sum_of(lgz, nz)).astype(BF)
    row_exchange(lambda q: lgs, lgt.at[:, col(j)], S_LGR)

    got(xr, S_X)

    @pl.loop(0, rw)
    def _(b):
        of = jnp.broadcast_to(slw[0:1, col(b)].astype(F32), (T, T))
        st[pl.ds(pl.multiple_of(b * T, T), T), :] = of.T
        lracc[b] = jnp.zeros((R, T), F32)

    def low_rank_chunk(yy):
        panels = dg[yy].reshape(rw * R, C)

        @pl.loop(0, rw // 2)
        def _(i):
            pair = xr[pl.ds(2 * i, 2)].reshape(2 * T, C)
            wide = lax.dot_general(panels, pair, NT, preferred_element_type=F32)
            for e in range(2):
                of = slw[0:1, col(2 * i + e)]
                total = lracc[2 * i + e]
                for k in range(rw):
                    total = total + jnp.where(
                        of == slot_id(k, yy), wide[k * R : (k + 1) * R, e * T : (e + 1) * T], 0.0
                    )
                lracc[2 * i + e] = total

    if ny > 2:
        ag_got(2)
    low_rank_chunk(y)

    got(lgt, S_LGR)

    def grad_chunk(yy):
        of = slw[0:1, :]
        lg = lgt[...].astype(F32)
        for k in range(rw):
            mbig[k * R : (k + 1) * R, :] = jnp.where(of == slot_id(k, yy), lg, 0.0).astype(BF)
        pa[yy] = jnp.dot(mbig[: rw * R, :], xr[...].reshape(rw * T, C), preferred_element_type=F32)

    def hrows(h):
        return pl.ds(h * hw * R, hw * R)

    def rs_copy(d, h, s):
        n = ring_steps(ny, d, h)
        dest = (y + (n - s + 1) if d == 0 else y - (n - s + 1)) % ny
        to = (y + 1 if d == 0 else y - 1) % ny
        return rcopy(
            pas.at[dest, hrows(h)], rb.at[d, h, s - 1], rs_s.at[d, h, s - 1], rs_r.at[d, h, s - 1], (y_dev(to), z)
        )

    def rs_send(d, h, s):
        n = ring_steps(ny, d, h)
        if s > n:
            return
        dest = (y + (n - s + 1) if d == 0 else y - (n - s + 1)) % ny
        part = pa[dest, hrows(h)]
        if s > 1:
            rs_got(d, h, s - 1)
            part = part + rb[d, h, s - 2].astype(F32)
        pas[dest, hrows(h)] = part.astype(BF)
        rs_copy(d, h, s).start()

    def rs_got(d, h, s):
        block = rb.at[d, h, s - 1]
        pltpu.make_async_copy(block, block, rs_r.at[d, h, s - 1]).wait()

    far = ny // 2
    grad_chunk((y + far) % ny)
    for d in range(2):
        rs_send(d, d, 1)
    if far > 1:
        grad_chunk((y + far - 1) % ny)
        grad_chunk((y - far + 1) % ny)
        for d in range(2):
            rs_send(d, 1 - d, 1)
    low_rank_chunk((y + 1) % ny)
    if ny > 2:
        low_rank_chunk((y - 1) % ny)
    for s in range(3, far + 1):
        ag_got(s)
    for s in range(2, far + 1):
        for d in range(2):
            rs_send(d, d, s)
        if far - s > 0:
            grad_chunk((y + far - s) % ny)
            grad_chunk((y - far + s) % ny)
            for d in range(2):
                rs_send(d, 1 - d, s)
    grad_chunk(y)
    for s in range(2, far):
        low_rank_chunk((y + s) % ny)
        low_rank_chunk((y - s) % ny)
    if far > 1:
        low_rank_chunk((y + far) % ny)

    @pl.loop(0, rw)
    def _(b):
        lrps[b] = lracc[b].astype(BF)

    row_exchange(lambda q: lrps.at[q], lrp.at[j], S_LRP)

    for h in range(2):
        total = pa[y, hrows(h)]
        for d in range(2):
            n = ring_steps(ny, d, h)
            if n > 0:
                rs_got(d, h, n)
                total = total + rb[d, h, n - 1].astype(F32)
        for k in range(hw):
            fin[h * hw + k] = total[k * R : (k + 1) * R]
    row_exchange(lambda q: fin.at[q], ga_out.at[:, col(j)], S_GA)

    got(lrp, S_LRP)
    lrzs[...] = sum_of(lrp, rw).astype(BF)
    z_exchange(lambda q: lrzs, lrz.at[z], S_LRZ)

    lane = lax.broadcasted_iota(jnp.int32, (T, 128), 1)

    def rows_of(b):
        return pl.ds(pl.multiple_of(b * T, T), T)

    def doubled(src):
        @pl.loop(0, rw)
        def _(b):
            one = src[:, col(b)].astype(F32)
            two[rows_of(b), :] = jnp.concatenate([one, one], axis=0).T

    def spread(ids):
        @pl.loop(0, rw)
        def _(b):
            of = st[rows_of(b), :]
            rows = two[rows_of(b), :]
            for m in range(len(ids) // 2):
                want = jnp.where(lane < R, ids[2 * m], ids[2 * m + 1]).astype(F32)
                mt[rows_of(b), m * 128 : (m + 1) * 128] = jnp.where(of == want, rows, 0.0).astype(BF)

    doubled(lgt)
    tgacc[...] = jnp.zeros_like(tgacc)

    @pl.loop(0, ny)
    def _(yy):
        spread([slot_id(k, yy) for k in range(rw)])
        tgacc[...] += jnp.dot(
            mt[:, : rw * R], dg[yy].reshape(rw * R, C), preferred_element_type=F32
        )

    tgs[...] = tgacc[...].astype(BF).reshape(rw, T, C)
    row_exchange(lambda q: tgs.at[q], tgc.at[j], S_TG)

    got(lrz, S_LRZ)
    lrs[...] = (2.0 * sum_of(lrz, nz)).astype(BF)
    row_exchange(lambda q: lrs, lrt.at[:, col(j)], S_LRR)

    got(tgc, S_TG)
    for k in range(rw):
        cols = slice(k * C, (k + 1) * C)
        tg_out[:, cols] = (fz[:, cols] + tgc[k].astype(F32)).astype(BF)

    got(lrt, S_LRR)
    doubled(lrt)
    spread([slot_id(j, yy) for yy in range(ny)])
    vcs[...] = (
        jnp.dot(mt[:, : ny * R], ug[...].reshape(ny * R, C), preferred_element_type=F32)
        .astype(BF)
        .reshape(rw, T, C)
    )
    row_exchange(lambda q: vcs.at[q], vc.at[j], S_VC)
    of = slw[0:1, :]
    lr = lrt[...].astype(F32)
    for yy in range(ny):
        mbig[yy * R : (yy + 1) * R, :] = jnp.where(of == slot_id(j, yy), lr, 0.0).astype(BF)
    pbs[...] = (
        jnp.dot(mbig[: ny * R, :], dyr[...].reshape(rw * T, C), preferred_element_type=F32)
        .astype(BF)
        .reshape(ny, R, C)
    )
    y_exchange(lambda q: pbs.at[q], gbp.at[y], S_GB)

    got(bz, S_BZ)
    got(vc, S_VC)
    v_out[...] = (sum_of(bz, nz) + sum_of(vc, rw)).astype(BF)
    got(gbp, S_GB)
    gb_out[...] = sum_of(gbp, ny)
    got(ga_out, S_GA)

    def sent(ref, stage):
        pltpu.make_async_copy(ref, ref, ss.at[stage]).wait()

    row = pl.ds(0, rw - 1)
    sent(dg.at[0, row], S_DT)
    sent(dyr.at[row], S_DY)
    sent(slw.at[:, pl.ds(0, (rw - 1) * 128)], S_SL)
    sent(xr.at[row], S_X)
    sent(dyf.at[:, pl.ds(0, (nz - 1) * 128)], S_DYZ)
    sent(ug.at[pl.ds(0, ny - 1)], S_U)
    sent(lgp.at[row], S_LGP)
    sent(lgz.at[pl.ds(0, nz - 1)], S_LGZ)
    sent(lgt.at[:, pl.ds(0, (rw - 1) * 128)], S_LGR)
    sent(bz.at[pl.ds(0, nz - 1)], S_BZ)
    sent(lrp.at[row], S_LRP)
    sent(lrz.at[pl.ds(0, nz - 1)], S_LRZ)
    sent(lrt.at[:, pl.ds(0, (rw - 1) * 128)], S_LRR)
    sent(tgc.at[row], S_TG)
    sent(vc.at[row], S_VC)
    sent(gbp.at[pl.ds(0, ny - 1)], S_GB)
    sent(fin.at[row], S_GA)
    for d in range(2):
        for h in range(2):
            for s in range(1, ring_steps(ny, d, h) + 1):
                ag_copy(d, h, s).wait_send()
                rs_copy(d, h, s).wait_send()


def shards(nx, ny, nz, tokens, weight, down, up, dy, adapter, lengths, table):
    rw = 2 * nx
    f = rw * C
    steps = max(1, ny // 2)
    hr = rw // 2 * R
    vm = pltpu.VMEM
    anywhere = pl.BlockSpec(memory_space=pl.ANY)
    vmem = pl.BlockSpec(memory_space=pltpu.VMEM)
    smem = pl.BlockSpec(memory_space=pltpu.SMEM)
    values, token_grad, grad_a, grad_b = pl.pallas_call(
        functools.partial(kernel, nx, ny, nz),
        out_shape=(
            jax.ShapeDtypeStruct((T, C), BF),
            jax.ShapeDtypeStruct((T, f), BF),
            jax.ShapeDtypeStruct((R, f), F32),
            jax.ShapeDtypeStruct((R, C), F32),
        ),
        in_specs=[anywhere] * 5 + [smem] * 3,
        out_specs=(vmem, vmem, vmem, vmem),
        scratch_shapes=[
            vm((T, f), BF),
            vm((f, nz * C), BF),
            vm((rw, T, C), BF),
            vm((ny, rw, R, C), BF),
            vm((rw, T, C), BF),
            vm((8, rw * T), jnp.int32),
            vm((8, T), jnp.int32),
            vm((T, nz * C), BF),
            vm((ny, R, C), BF),
            vm((rw, R, T), BF),
            vm((rw, R, T), BF),
            vm((R, T), BF),
            vm((nz, R, T), BF),
            vm((R, T), BF),
            vm((R, rw * T), BF),
            vm((nz, T, C), BF),
            vm((nz, T, C), BF),
            vm((T, f), F32),
            vm((rw, R, T), F32),
            vm((rw, R, T), BF),
            vm((rw, R, T), BF),
            vm((R, T), BF),
            vm((nz, R, T), BF),
            vm((R, T), BF),
            vm((R, rw * T), BF),
            vm((max(rw, ny) * R, rw * T), BF),
            vm((rw * T, max(rw, ny) * R), BF),
            vm((rw * T, 128), F32),
            vm((rw * T, 128), F32),
            vm((rw * T, C), F32),
            vm((rw, T, C), BF),
            vm((rw, T, C), BF),
            vm((rw, T, C), BF),
            vm((rw, T, C), BF),
            vm((ny, R, C), BF),
            vm((ny, R, C), BF),
            vm((ny, rw * R, C), F32),
            vm((ny, rw * R, C), BF),
            vm((2, 2, steps, hr, C), BF),
            vm((rw, R, C), F32),
            pltpu.SemaphoreType.DMA((N_STAGES,)),
            pltpu.SemaphoreType.DMA((N_STAGES,)),
            pltpu.SemaphoreType.DMA((2, 2, steps)),
            pltpu.SemaphoreType.DMA((2, 2, steps)),
            pltpu.SemaphoreType.DMA((2, 2, steps)),
            pltpu.SemaphoreType.DMA((2, 2, steps)),
            pltpu.SemaphoreType.DMA((2,)),
        ],
        compiler_params=pltpu.CompilerParams(
            collective_id=0, has_side_effects=True, vmem_limit_bytes=48 * 1024 * 1024
        ),
    )(
        tokens,
        weight,
        jnp.swapaxes(down[0], 0, 1),
        up[0],
        dy,
        adapter.reshape(-1),
        lengths.reshape(-1),
        table,
    )
    return values, token_grad, jnp.swapaxes(grad_a, 0, 1)[None], grad_b[None]


def solution(mesh, nx=4):
    dp, nz = mesh.shape["dp"], mesh.shape["tensor"]
    return jax.shard_map(
        functools.partial(shards, nx, dp // (2 * nx), nz),
        mesh=mesh,
        in_specs=(
            P("dp", "tensor"),
            P("tensor", None),
            P("dp", "tensor", None),
            P("dp", None, "tensor"),
            P("dp", "tensor"),
            P("dp", None),
            P("dp", None),
            P(),
        ),
        out_specs=(
            P("dp", "tensor"),
            P("dp", "tensor"),
            P("dp", "tensor", None),
            P("dp", None, "tensor"),
        ),
        check_vma=False,
    )
```

```python
import functools

import jax
import jax.numpy as jnp
from jax import lax
from jax.experimental import pallas as pl
from jax.experimental.pallas import tpu as pltpu
from jax.sharding import PartitionSpec as P

LIMIT = 56 * 1024 * 1024
MESH = pl.DeviceIdType.MESH
BF = jnp.bfloat16
F32 = jnp.float32
NT = (((1,), (1,)), ((), ()))
T = 128
R = 64
C = 128

(S_DT, S_DY, S_SL, S_X, S_DYZ, S_U, S_LGP, S_LGZ, S_LGR, S_BZ, S_LRP, S_LRZ, S_LRR, S_TG, S_VC, S_GB, S_GA) = range(17)
N_STAGES = 17


def ring_steps(ny, d, h):
    return ny // 2 if d == h else ny - 1 - ny // 2


def kernel(
    nx, ny, nz,
    x_hbm, w_hbm, dt_hbm, u_hbm, dy_hbm, adp, lens, tab,
    v_out, tg_out, ga_out, gb_out,
    xv, wv, xr, dg, dyr, slw, slo, dyf, ug,
    lgps, lgp, lgzs, lgz, lgs, lgt,
    bs, bz, fz,
    lracc, lrps, lrp, lrzs, lrz, lrs, lrt,
    mbig, mt, two, st, tgacc, tgs, tgc, vcs, vc, pbs, gbp,
    pa, pas, rb, fin,
    ss, rs, ag_s, ag_r, rs_s, rs_r, ld,
):
    rw = 2 * nx
    hw = rw // 2
    me = lax.axis_index("dp")
    z = lax.axis_index("tensor")
    c = me % 2
    y = (me // 2) % ny
    x = me // (2 * ny)
    j = x * 2 + c

    def row_dev(jj):
        odd = lax.rem(jj, 2)
        return ny * (jj - odd) + odd + 2 * y

    def y_dev(yy):
        return x * (2 * ny) + yy * 2 + c

    def slot_id(jj, yy):
        return (jj // 2) * (2 * ny) + yy * 2 + jj % 2

    def col(i):
        return pl.ds(pl.multiple_of(i * 128, 128), 128)

    row = pl.ds(0, rw - 1)
    row_cols = pl.ds(0, (rw - 1) * 128)
    zs = pl.ds(0, nz - 1)
    ys = pl.ds(0, ny - 1)
    arrives = {
        S_DT: (dg.at[y], dg.at[0, row]),
        S_DY: (dyr, dyr.at[row]),
        S_SL: (slw, slw.at[:, row_cols]),
        S_X: (xr, xr.at[row]),
        S_DYZ: (dyf, dyf.at[:, pl.ds(0, (nz - 1) * 128)]),
        S_U: (ug, ug.at[ys]),
        S_LGP: (lgp, lgp.at[row]),
        S_LGZ: (lgz, lgz.at[zs]),
        S_LGR: (lgt, lgt.at[:, row_cols]),
        S_BZ: (bz, bz.at[zs]),
        S_LRP: (lrp, lrp.at[row]),
        S_LRZ: (lrz, lrz.at[zs]),
        S_LRR: (lrt, lrt.at[:, row_cols]),
        S_TG: (tgc, tgc.at[row]),
        S_VC: (vc, vc.at[row]),
        S_GB: (gbp, gbp.at[ys]),
        S_GA: (ga_out, fin.at[row]),
    }
    started, done = [], []

    def rcopy(src, dst, s, r, dev):
        return pltpu.make_async_remote_copy(
            src_ref=src, dst_ref=dst, send_sem=s, recv_sem=r, device_id=dev, device_id_type=MESH
        )

    def exchange(n, mine, dev, src, dst, stage):
        @pl.loop(1, n)
        def _(i):
            q = lax.rem(mine + i, n)
            rcopy(src(q), dst, ss.at[stage], rs.at[stage], dev(q)).start()

        pltpu.make_async_copy(src(mine), dst, rs.at[stage]).start()
        started.append(stage)

    def row_exchange(src, dst, stage):
        exchange(rw, j, lambda q: (row_dev(q), z), src, dst, stage)

    def y_exchange(src, dst, stage):
        exchange(ny, y, lambda q: (y_dev(q), z), src, dst, stage)

    def z_exchange(src, dst, stage):
        exchange(nz, z, lambda q: (me, q), src, dst, stage)

    def got(stage):
        ref = arrives[stage][0]
        pltpu.make_async_copy(ref, ref, rs.at[stage]).wait()
        done.append(stage)

    barrier = pltpu.get_barrier_semaphore()

    @pl.loop(1, rw)
    def _(i):
        pl.semaphore_signal(barrier, inc=1, device_id=(row_dev((j + i) % rw), z), device_id_type=MESH)

    @pl.loop(1, ny)
    def _(i):
        pl.semaphore_signal(barrier, inc=1, device_id=(y_dev((y + i) % ny), z), device_id_type=MESH)

    @pl.loop(1, nz)
    def _(i):
        pl.semaphore_signal(barrier, inc=1, device_id=(me, (z + i) % nz), device_id_type=MESH)

    load_w = pltpu.make_async_copy(w_hbm, wv, ld.at[0])
    load_x = pltpu.make_async_copy(x_hbm, xv, ld.at[1])
    load_x.start()
    load_w.start()

    position = lax.broadcasted_iota(jnp.int32, (8, T), 1)
    slots = jnp.full((8, T), 0, jnp.int32)
    begin = jnp.int32(0)
    for k in range(8):
        slots = jnp.where(position >= begin, tab[adp[k]], slots)
        begin = begin + lens[k]
    slo[...] = slots

    def work():
        pl.semaphore_wait(barrier, rw + ny + nz - 3)

        row_exchange(lambda q: dt_hbm.at[:, col(q)], dg.at[y, j], S_DT)
        y_exchange(lambda q: u_hbm, ug.at[y], S_U)
        row_exchange(lambda q: slo, slw.at[:, col(j)], S_SL)
        row_exchange(lambda q: dy_hbm, dyr.at[j], S_DY)
        z_exchange(lambda q: dy_hbm, dyf.at[:, col(z)], S_DYZ)
        row_exchange(lambda q: x_hbm.at[:, col(q)], xr.at[j], S_X)

        def half(h):
            return pl.ds(h * hw, hw)

        def ag_copy(d, h, s):
            yy = (y - (s - 1) if d == 0 else y + (s - 1)) % ny
            to = (y + 1 if d == 0 else y - 1) % ny
            block = dg.at[yy, half(h)]
            return rcopy(block, block, ag_s.at[d, h, s - 1], ag_r.at[d, h, s - 1], (y_dev(to), z))

        def ag_send(s):
            for h in range(2):
                for d in range(2):
                    if s <= ring_steps(ny, d, h):
                        started.append((ag_copy, d, h, s))
                        ag_copy(d, h, s).start()

        def ag_got(s):
            for h in range(2):
                for d in range(2):
                    if s <= ring_steps(ny, d, h):
                        ag_copy(d, h, s).wait_recv()
                        done.append((ag_copy, d, h, s))
                        if s + 1 <= ring_steps(ny, d, h):
                            started.append((ag_copy, d, h, s + 1))
                            ag_copy(d, h, s + 1).start()

        def sum_of(ref, n):
            total = ref[0].astype(F32)
            for i in range(1, n):
                total = total + ref[i].astype(F32)
            return total

        def low_rank_chunk(yy):
            panels = dg[yy].reshape(rw * R, C)

            @pl.loop(0, rw // 2)
            def _(i):
                pair = xr[pl.ds(2 * i, 2)].reshape(2 * T, C)
                wide = lax.dot_general(panels, pair, NT, preferred_element_type=F32)
                for e in range(2):
                    of = slw[0:1, col(2 * i + e)]
                    total = lracc[2 * i + e]
                    for k in range(rw):
                        total = total + jnp.where(
                            of == slot_id(k, yy), wide[k * R : (k + 1) * R, e * T : (e + 1) * T], 0.0
                        )
                    lracc[2 * i + e] = total

        def grad_chunk(yy):
            of = slw[0:1, :]
            lg = lgt[...].astype(F32)
            for k in range(rw):
                mbig[k * R : (k + 1) * R, :] = jnp.where(of == slot_id(k, yy), lg, 0.0).astype(BF)
            pa[yy] = jnp.dot(mbig[: rw * R, :], xr[...].reshape(rw * T, C), preferred_element_type=F32)

        def hrows(h):
            return pl.ds(h * hw * R, hw * R)

        def rs_copy(d, h, s):
            n = ring_steps(ny, d, h)
            dest = (y + (n - s + 1) if d == 0 else y - (n - s + 1)) % ny
            to = (y + 1 if d == 0 else y - 1) % ny
            return rcopy(
                pas.at[dest, hrows(h)], rb.at[d, h, s - 1], rs_s.at[d, h, s - 1], rs_r.at[d, h, s - 1], (y_dev(to), z)
            )

        def rs_send(d, h, s):
            n = ring_steps(ny, d, h)
            if s > n:
                return
            dest = (y + (n - s + 1) if d == 0 else y - (n - s + 1)) % ny
            part = pa[dest, hrows(h)]
            if s > 1:
                rs_got(d, h, s - 1)
                part = part + rb[d, h, s - 2].astype(F32)
            pas[dest, hrows(h)] = part.astype(BF)
            started.append((rs_copy, d, h, s))
            rs_copy(d, h, s).start()

        def rs_got(d, h, s):
            rs_copy(d, h, s).wait_recv()
            done.append((rs_copy, d, h, s))

        far = ny // 2

        def rs_step(s):
            for d in range(2):
                rs_send(d, d, s)
            for d in range(2):
                rs_send(d, 1 - d, s)

        def both(step, distance):
            step((y + distance) % ny)
            step((y - distance) % ny)

        lane = lax.broadcasted_iota(jnp.int32, (T, 128), 1)

        def rows_of(b):
            return pl.ds(pl.multiple_of(b * T, T), T)

        def doubled(src):
            @pl.loop(0, rw)
            def _(b):
                one = src[:, col(b)].astype(F32)
                two[rows_of(b), :] = jnp.concatenate([one, one], axis=0).T

        def spread(ids):
            @pl.loop(0, rw)
            def _(b):
                of = st[rows_of(b), :]
                rows = two[rows_of(b), :]
                for m in range(len(ids) // 2):
                    want = jnp.where(lane < R, ids[2 * m], ids[2 * m + 1]).astype(F32)
                    mt[rows_of(b), m * 128 : (m + 1) * 128] = jnp.where(of == want, rows, 0.0).astype(BF)

        load_x.wait()
        load_w.wait()

        @pl.loop(0, nz // 2)
        def _(i):
            part = jnp.dot(
                xv[...], wv[:, pl.ds(pl.multiple_of(i * 256, 256), 256)], preferred_element_type=F32
            ).astype(BF)
            bs[2 * i] = part[:, :C]
            bs[2 * i + 1] = part[:, C:]

        got(S_DT)
        ag_send(1)

        got(S_U)
        got(S_SL)
        got(S_DY)

        @pl.loop(0, rw)
        def _(b):
            wide = lax.dot_general(
                ug[...].reshape(ny * R, C), dyr[b], NT, preferred_element_type=F32
            )
            of = slw[0:1, col(b)]
            total = jnp.zeros((R, T), F32)
            for yy in range(ny):
                total = total + jnp.where(of == slot_id(j, yy), wide[yy * R : (yy + 1) * R], 0.0)
            lgps[b] = total.astype(BF)

        row_exchange(lambda q: lgps.at[q], lgp.at[j], S_LGP)

        @pl.loop(0, rw)
        def _(b):
            of = jnp.broadcast_to(slw[0:1, col(b)].astype(F32), (T, T))
            st[pl.ds(pl.multiple_of(b * T, T), T), :] = of.T
            lracc[b] = jnp.zeros((R, T), F32)

        ag_got(1)
        got(S_LGP)
        lgzs[...] = sum_of(lgp, rw).astype(BF)
        z_exchange(lambda q: lgzs, lgz.at[z], S_LGZ)

        got(S_X)
        low_rank_chunk(y)
        if far > 1:
            ag_got(2)

        got(S_LGZ)
        lgs[...] = (2.0 * sum_of(lgz, nz)).astype(BF)
        row_exchange(lambda q: lgs, lgt.at[:, col(j)], S_LGR)
        z_exchange(lambda q: bs.at[q], bz.at[z], S_BZ)

        if far > 1:
            both(low_rank_chunk, 1)
        if far > 2:
            ag_got(3)

        got(S_DYZ)

        @pl.loop(0, rw // 2)
        def _(i):
            f = pl.ds(pl.multiple_of(i * 256, 256), 256)
            fz[:, f] = lax.dot_general(dyf[...], wv[f, :], NT, preferred_element_type=F32)

        got(S_LGR)
        grad_chunk((y + far) % ny)
        for d in range(2):
            rs_send(d, d, 1)
        if far > 1:
            both(grad_chunk, far - 1)
            for d in range(2):
                rs_send(d, 1 - d, 1)
        for s in range(4, far + 1):
            ag_got(s)
        for s in range(2, far):
            both(low_rank_chunk, s)
        low_rank_chunk((y + far) % ny)

        @pl.loop(0, rw)
        def _(b):
            lrps[b] = lracc[b].astype(BF)

        row_exchange(lambda q: lrps.at[q], lrp.at[j], S_LRP)

        for s in range(2, far):
            both(grad_chunk, far - s)
        if far > 1:
            rs_step(2)
        doubled(lgt)
        grad_chunk(y)

        got(S_LRP)
        lrzs[...] = sum_of(lrp, rw).astype(BF)
        z_exchange(lambda q: lrzs, lrz.at[z], S_LRZ)

        if far > 2:
            rs_step(3)
        tgacc[...] = jnp.zeros_like(tgacc)

        @pl.loop(0, ny)
        def _(yy):
            spread([slot_id(k, yy) for k in range(rw)])
            tgacc[...] += jnp.dot(
                mt[:, : rw * R], dg[yy].reshape(rw * R, C), preferred_element_type=F32
            )

        tgs[...] = tgacc[...].astype(BF).reshape(rw, T, C)
        row_exchange(lambda q: tgs.at[q], tgc.at[j], S_TG)

        got(S_LRZ)
        lrs[...] = (2.0 * sum_of(lrz, nz)).astype(BF)
        row_exchange(lambda q: lrs, lrt.at[:, col(j)], S_LRR)

        for s in range(4, far + 1):
            rs_step(s)
        for h in range(2):
            total = pa[y, hrows(h)]
            for d in range(2):
                n = ring_steps(ny, d, h)
                if n > 0:
                    rs_got(d, h, n)
                    total = total + rb[d, h, n - 1].astype(F32)
            for k in range(hw):
                fin[h * hw + k] = total[k * R : (k + 1) * R]
        row_exchange(lambda q: fin.at[q], ga_out.at[:, col(j)], S_GA)

        got(S_LRR)
        of = slw[0:1, :]
        lr = lrt[...].astype(F32)
        for yy in range(ny):
            mbig[yy * R : (yy + 1) * R, :] = jnp.where(of == slot_id(j, yy), lr, 0.0).astype(BF)
        pbs[...] = (
            jnp.dot(mbig[: ny * R, :], dyr[...].reshape(rw * T, C), preferred_element_type=F32)
            .astype(BF)
            .reshape(ny, R, C)
        )
        y_exchange(lambda q: pbs.at[q], gbp.at[y], S_GB)
        doubled(lrt)
        spread([slot_id(j, yy) for yy in range(ny)])
        vcs[...] = (
            jnp.dot(mt[:, : ny * R], ug[...].reshape(ny * R, C), preferred_element_type=F32)
            .astype(BF)
            .reshape(rw, T, C)
        )
        row_exchange(lambda q: vcs.at[q], vc.at[j], S_VC)

        got(S_TG)
        for k in range(rw):
            cols = slice(k * C, (k + 1) * C)
            tg_out[:, cols] = (fz[:, cols] + tgc[k].astype(F32)).astype(BF)
        got(S_BZ)
        got(S_VC)
        v_out[...] = (sum_of(bz, nz) + sum_of(vc, rw)).astype(BF)
        got(S_GB)
        gb_out[...] = sum_of(gbp, ny)
        got(S_GA)

    work()

    for one in started:
        if isinstance(one, tuple):
            if one not in done:
                one[0](*one[1:]).wait_recv()
            one[0](*one[1:]).wait_send()
        else:
            if one not in done:
                got(one)
            ref = arrives[one][1]
            pltpu.make_async_copy(ref, ref, ss.at[one]).wait()


def shards(nx, ny, nz, tokens, weight, down, up, dy, adapter, lengths, table):
    rw = 2 * nx
    f = rw * C
    steps = max(1, ny // 2)
    hr = rw // 2 * R
    vm = pltpu.VMEM
    anywhere = pl.BlockSpec(memory_space=pl.ANY)
    vmem = pl.BlockSpec(memory_space=pltpu.VMEM)
    smem = pl.BlockSpec(memory_space=pltpu.SMEM)
    values, token_grad, grad_a, grad_b = pl.pallas_call(
        functools.partial(kernel, nx, ny, nz),
        out_shape=(
            jax.ShapeDtypeStruct((T, C), BF),
            jax.ShapeDtypeStruct((T, f), BF),
            jax.ShapeDtypeStruct((R, f), F32),
            jax.ShapeDtypeStruct((R, C), F32),
        ),
        in_specs=[anywhere] * 5 + [smem] * 3,
        out_specs=(vmem, vmem, vmem, vmem),
        scratch_shapes=[
            vm((T, f), BF),
            vm((f, nz * C), BF),
            vm((rw, T, C), BF),
            vm((ny, rw, R, C), BF),
            vm((rw, T, C), BF),
            vm((8, rw * T), jnp.int32),
            vm((8, T), jnp.int32),
            vm((T, nz * C), BF),
            vm((ny, R, C), BF),
            vm((rw, R, T), BF),
            vm((rw, R, T), BF),
            vm((R, T), BF),
            vm((nz, R, T), BF),
            vm((R, T), BF),
            vm((R, rw * T), BF),
            vm((nz, T, C), BF),
            vm((nz, T, C), BF),
            vm((T, f), F32),
            vm((rw, R, T), F32),
            vm((rw, R, T), BF),
            vm((rw, R, T), BF),
            vm((R, T), BF),
            vm((nz, R, T), BF),
            vm((R, T), BF),
            vm((R, rw * T), BF),
            vm((max(rw, ny) * R, rw * T), BF),
            vm((rw * T, max(rw, ny) * R), BF),
            vm((rw * T, 128), F32),
            vm((rw * T, 128), F32),
            vm((rw * T, C), F32),
            vm((rw, T, C), BF),
            vm((rw, T, C), BF),
            vm((rw, T, C), BF),
            vm((rw, T, C), BF),
            vm((ny, R, C), BF),
            vm((ny, R, C), BF),
            vm((ny, rw * R, C), F32),
            vm((ny, rw * R, C), BF),
            vm((2, 2, steps, hr, C), BF),
            vm((rw, R, C), F32),
            pltpu.SemaphoreType.DMA((N_STAGES,)),
            pltpu.SemaphoreType.DMA((N_STAGES,)),
            pltpu.SemaphoreType.DMA((2, 2, steps)),
            pltpu.SemaphoreType.DMA((2, 2, steps)),
            pltpu.SemaphoreType.DMA((2, 2, steps)),
            pltpu.SemaphoreType.DMA((2, 2, steps)),
            pltpu.SemaphoreType.DMA((2,)),
        ],
        compiler_params=pltpu.CompilerParams(
            collective_id=0, has_side_effects=True, vmem_limit_bytes=LIMIT
        ),
    )(
        tokens,
        weight,
        jnp.swapaxes(down[0], 0, 1),
        up[0],
        dy,
        adapter.reshape(-1),
        lengths.reshape(-1),
        table,
    )
    return values, token_grad, jnp.swapaxes(grad_a, 0, 1)[None], grad_b[None]


def solution(mesh, nx=4):
    dp, nz = mesh.shape["dp"], mesh.shape["tensor"]
    return jax.shard_map(
        functools.partial(shards, nx, dp // (2 * nx), nz),
        mesh=mesh,
        in_specs=(
            P("dp", "tensor"),
            P("tensor", None),
            P("dp", "tensor", None),
            P("dp", None, "tensor"),
            P("dp", "tensor"),
            P("dp", None),
            P("dp", None),
            P(),
        ),
        out_specs=(
            P("dp", "tensor"),
            P("dp", "tensor"),
            P("dp", "tensor", None),
            P("dp", None, "tensor"),
        ),
        check_vma=False,
    )
```

```python
import functools

import jax
import jax.numpy as jnp
from jax import lax
from jax.experimental import pallas as pl
from jax.experimental.pallas import tpu as pltpu
from jax.sharding import PartitionSpec as P

LIMIT = 56 * 1024 * 1024
MESH = pl.DeviceIdType.MESH
BF = jnp.bfloat16
F32 = jnp.float32
NT = (((1,), (1,)), ((), ()))
T = 128
R = 64
C = 128

(S_DT, S_DY, S_SL, S_X, S_DYZ, S_U, S_LGP, S_LGZ, S_LGR, S_BZ, S_LRP, S_LRZ, S_LRR, S_TG, S_VC, S_GB, S_GA) = range(17)
N_STAGES = 17


def ring_steps(ny, d, h):
    return ny // 2 if d == h else ny - 1 - ny // 2


def kernel(
    nx, ny, nz,
    x_hbm, w_hbm, dt_hbm, u_hbm, dy_hbm, adp, lens, tab,
    v_out, tg_out, ga_out, gb_out,
    xv, wv, xr, dg, dyr, slw, slo, dyf, ug,
    lgps, lgp, lgzs, lgz, lgs, lgt,
    bs, bz, fz,
    lracc, lrps, lrp, lrzs, lrz, lrs, lrt,
    mbig, mt, two, st, tgacc, tgs, tgc, vcs, vc, pbs, gbp,
    pa, pas, rb, fin, gar,
    ss, rs, ag_s, ag_r, rs_s, rs_r, ld,
):
    rw = 2 * nx
    hw = rw // 2
    me = lax.axis_index("dp")
    z = lax.axis_index("tensor")
    c = me % 2
    y = (me // 2) % ny
    x = me // (2 * ny)
    j = x * 2 + c

    def row_dev(jj):
        odd = lax.rem(jj, 2)
        return ny * (jj - odd) + odd + 2 * y

    def y_dev(yy):
        return x * (2 * ny) + yy * 2 + c

    def slot_id(jj, yy):
        return (jj // 2) * (2 * ny) + yy * 2 + jj % 2

    def col(i):
        return pl.ds(pl.multiple_of(i * 128, 128), 128)

    row = pl.ds(0, rw - 1)
    row_cols = pl.ds(0, (rw - 1) * 128)
    zs = pl.ds(0, nz - 1)
    ys = pl.ds(0, ny - 1)
    arrives = {
        S_DT: (dg.at[y], dg.at[0, row]),
        S_DY: (dyr, dyr.at[row]),
        S_SL: (slw, slw.at[:, row_cols]),
        S_X: (xr, xr.at[row]),
        S_DYZ: (dyf, dyf.at[:, pl.ds(0, (nz - 1) * 128)]),
        S_U: (ug, ug.at[ys]),
        S_LGP: (lgp, lgp.at[row]),
        S_LGZ: (lgz, lgz.at[zs]),
        S_LGR: (lgt, lgt.at[:, row_cols]),
        S_BZ: (bz, bz.at[zs]),
        S_LRP: (lrp, lrp.at[row]),
        S_LRZ: (lrz, lrz.at[zs]),
        S_LRR: (lrt, lrt.at[:, row_cols]),
        S_TG: (tgc, tgc.at[row]),
        S_VC: (vc, vc.at[row]),
        S_GB: (gbp, gbp.at[ys]),
        S_GA: (gar, fin.at[row]),
    }
    started, done = [], []

    def rcopy(src, dst, s, r, dev):
        return pltpu.make_async_remote_copy(
            src_ref=src, dst_ref=dst, send_sem=s, recv_sem=r, device_id=dev, device_id_type=MESH
        )

    def exchange(n, mine, dev, src, dst, stage):
        @pl.loop(1, n)
        def _(i):
            q = lax.rem(mine + i, n)
            rcopy(src(q), dst, ss.at[stage], rs.at[stage], dev(q)).start()

        pltpu.make_async_copy(src(mine), dst, rs.at[stage]).start()
        started.append(stage)

    def row_exchange(src, dst, stage):
        exchange(rw, j, lambda q: (row_dev(q), z), src, dst, stage)

    def y_exchange(src, dst, stage):
        exchange(ny, y, lambda q: (y_dev(q), z), src, dst, stage)

    def z_exchange(src, dst, stage):
        exchange(nz, z, lambda q: (me, q), src, dst, stage)

    def got(stage):
        ref = arrives[stage][0]
        pltpu.make_async_copy(ref, ref, rs.at[stage]).wait()
        done.append(stage)

    barrier = pltpu.get_barrier_semaphore()

    @pl.loop(1, rw)
    def _(i):
        pl.semaphore_signal(barrier, inc=1, device_id=(row_dev((j + i) % rw), z), device_id_type=MESH)

    @pl.loop(1, ny)
    def _(i):
        pl.semaphore_signal(barrier, inc=1, device_id=(y_dev((y + i) % ny), z), device_id_type=MESH)

    @pl.loop(1, nz)
    def _(i):
        pl.semaphore_signal(barrier, inc=1, device_id=(me, (z + i) % nz), device_id_type=MESH)

    load_w = pltpu.make_async_copy(w_hbm, wv, ld.at[0])
    load_x = pltpu.make_async_copy(x_hbm, xv, ld.at[1])
    load_x.start()
    load_w.start()

    position = lax.broadcasted_iota(jnp.int32, (8, T), 1)
    slots = jnp.full((8, T), 0, jnp.int32)
    begin = jnp.int32(0)
    for k in range(8):
        slots = jnp.where(position >= begin, tab[adp[k]], slots)
        begin = begin + lens[k]
    slo[...] = slots

    def work():
        pl.semaphore_wait(barrier, rw + ny + nz - 3)

        row_exchange(lambda q: dt_hbm.at[:, col(q)], dg.at[y, j], S_DT)
        y_exchange(lambda q: u_hbm, ug.at[y], S_U)
        row_exchange(lambda q: slo, slw.at[:, col(j)], S_SL)
        row_exchange(lambda q: dy_hbm, dyr.at[j], S_DY)
        z_exchange(lambda q: dy_hbm, dyf.at[:, col(z)], S_DYZ)
        row_exchange(lambda q: x_hbm.at[:, col(q)], xr.at[j], S_X)

        def half(h):
            return pl.ds(h * hw, hw)

        def ag_copy(d, h, s):
            yy = (y - (s - 1) if d == 0 else y + (s - 1)) % ny
            to = (y + 1 if d == 0 else y - 1) % ny
            block = dg.at[yy, half(h)]
            return rcopy(block, block, ag_s.at[d, h, s - 1], ag_r.at[d, h, s - 1], (y_dev(to), z))

        def ag_send(s):
            for h in range(2):
                for d in range(2):
                    if s <= ring_steps(ny, d, h):
                        started.append((ag_copy, d, h, s))
                        ag_copy(d, h, s).start()

        def ag_got(s):
            for h in range(2):
                for d in range(2):
                    if s <= ring_steps(ny, d, h):
                        ag_copy(d, h, s).wait_recv()
                        done.append((ag_copy, d, h, s))
                        if s + 1 <= ring_steps(ny, d, h):
                            started.append((ag_copy, d, h, s + 1))
                            ag_copy(d, h, s + 1).start()

        def sum_of(ref, n):
            total = ref[0].astype(F32)
            for i in range(1, n):
                total = total + ref[i].astype(F32)
            return total

        def low_rank_chunk(yy):
            panels = dg[yy].reshape(rw * R, C)

            @pl.loop(0, rw // 2)
            def _(i):
                pair = xr[pl.ds(2 * i, 2)].reshape(2 * T, C)
                wide = lax.dot_general(panels, pair, NT, preferred_element_type=F32)
                for e in range(2):
                    of = slw[0:1, col(2 * i + e)]
                    total = lracc[2 * i + e]
                    for k in range(rw):
                        total = total + jnp.where(
                            of == slot_id(k, yy), wide[k * R : (k + 1) * R, e * T : (e + 1) * T], 0.0
                        )
                    lracc[2 * i + e] = total

        def grad_chunk(yy):
            of = slw[0:1, :]
            lg = lgt[...].astype(F32)
            for k in range(rw):
                mbig[k * R : (k + 1) * R, :] = jnp.where(of == slot_id(k, yy), lg, 0.0).astype(BF)
            pa[yy] = jnp.dot(mbig[: rw * R, :], xr[...].reshape(rw * T, C), preferred_element_type=F32)

        def hrows(h):
            return pl.ds(h * hw * R, hw * R)

        def rs_copy(d, h, s):
            n = ring_steps(ny, d, h)
            dest = (y + (n - s + 1) if d == 0 else y - (n - s + 1)) % ny
            to = (y + 1 if d == 0 else y - 1) % ny
            return rcopy(
                pas.at[dest, hrows(h)], rb.at[d, h, s - 1], rs_s.at[d, h, s - 1], rs_r.at[d, h, s - 1], (y_dev(to), z)
            )

        def rs_send(d, h, s):
            n = ring_steps(ny, d, h)
            if s > n:
                return
            dest = (y + (n - s + 1) if d == 0 else y - (n - s + 1)) % ny
            part = pa[dest, hrows(h)]
            if s > 1:
                rs_got(d, h, s - 1)
                part = part + rb[d, h, s - 2].astype(F32)
            pas[dest, hrows(h)] = part.astype(BF)
            started.append((rs_copy, d, h, s))
            rs_copy(d, h, s).start()

        def rs_got(d, h, s):
            rs_copy(d, h, s).wait_recv()
            done.append((rs_copy, d, h, s))

        far = ny // 2

        def rs_step(s):
            for d in range(2):
                rs_send(d, d, s)
            for d in range(2):
                rs_send(d, 1 - d, s)

        def both(step, distance):
            step((y + distance) % ny)
            step((y - distance) % ny)

        lane = lax.broadcasted_iota(jnp.int32, (T, 128), 1)

        def rows_of(b):
            return pl.ds(pl.multiple_of(b * T, T), T)

        def doubled(src):
            @pl.loop(0, rw)
            def _(b):
                one = src[:, col(b)].astype(F32)
                two[rows_of(b), :] = jnp.concatenate([one, one], axis=0).T

        def spread(ids):
            @pl.loop(0, rw)
            def _(b):
                of = st[rows_of(b), :]
                rows = two[rows_of(b), :]
                for m in range(len(ids) // 2):
                    want = jnp.where(lane < R, ids[2 * m], ids[2 * m + 1]).astype(F32)
                    mt[rows_of(b), m * 128 : (m + 1) * 128] = jnp.where(of == want, rows, 0.0).astype(BF)

        load_x.wait()
        load_w.wait()

        @pl.loop(0, nz // 2)
        def _(i):
            part = jnp.dot(
                xv[...], wv[:, pl.ds(pl.multiple_of(i * 256, 256), 256)], preferred_element_type=F32
            ).astype(BF)
            bs[2 * i] = part[:, :C]
            bs[2 * i + 1] = part[:, C:]

        got(S_DT)
        ag_send(1)

        got(S_U)
        got(S_SL)
        got(S_DY)

        @pl.loop(0, rw)
        def _(b):
            wide = lax.dot_general(
                ug[...].reshape(ny * R, C), dyr[b], NT, preferred_element_type=F32
            )
            of = slw[0:1, col(b)]
            total = jnp.zeros((R, T), F32)
            for yy in range(ny):
                total = total + jnp.where(of == slot_id(j, yy), wide[yy * R : (yy + 1) * R], 0.0)
            lgps[b] = total.astype(BF)

        row_exchange(lambda q: lgps.at[q], lgp.at[j], S_LGP)

        @pl.loop(0, rw)
        def _(b):
            of = jnp.broadcast_to(slw[0:1, col(b)].astype(F32), (T, T))
            st[pl.ds(pl.multiple_of(b * T, T), T), :] = of.T
            lracc[b] = jnp.zeros((R, T), F32)

        ag_got(1)
        got(S_LGP)
        lgzs[...] = sum_of(lgp, rw).astype(BF)
        z_exchange(lambda q: lgzs, lgz.at[z], S_LGZ)

        got(S_X)
        low_rank_chunk(y)
        if far > 1:
            ag_got(2)
            both(low_rank_chunk, 1)

        got(S_DYZ)

        @pl.loop(0, rw // 2)
        def _(i):
            f = pl.ds(pl.multiple_of(i * 256, 256), 256)
            fz[:, f] = lax.dot_general(dyf[...], wv[f, :], NT, preferred_element_type=F32)

        if far > 2:
            ag_got(3)
        if far > 2:
            both(low_rank_chunk, 2)

        got(S_LGZ)
        lgs[...] = (2.0 * sum_of(lgz, nz)).astype(BF)
        row_exchange(lambda q: lgs, lgt.at[:, col(j)], S_LGR)

        for s in range(4, far + 1):
            ag_got(s)
        for s in range(3, far):
            both(low_rank_chunk, s)
        low_rank_chunk((y + far) % ny)

        @pl.loop(0, rw)
        def _(b):
            lrps[b] = lracc[b].astype(BF)

        row_exchange(lambda q: lrps.at[q], lrp.at[j], S_LRP)

        got(S_LGR)
        grad_chunk((y + far) % ny)
        for d in range(2):
            rs_send(d, d, 1)
        if far > 1:
            both(grad_chunk, far - 1)
            for d in range(2):
                rs_send(d, 1 - d, 1)

        got(S_LRP)
        lrzs[...] = sum_of(lrp, rw).astype(BF)
        z_exchange(lambda q: lrzs, lrz.at[z], S_LRZ)
        z_exchange(lambda q: bs.at[q], bz.at[z], S_BZ)

        for s in range(2, far):
            both(grad_chunk, far - s)
        if far > 1:
            rs_step(2)
        doubled(lgt)
        tgacc[...] = jnp.zeros_like(tgacc)

        @pl.loop(0, ny)
        def _(yy):
            spread([slot_id(k, yy) for k in range(rw)])
            tgacc[...] += jnp.dot(
                mt[:, : rw * R], dg[yy].reshape(rw * R, C), preferred_element_type=F32
            )

        tgs[...] = tgacc[...].astype(BF).reshape(rw, T, C)
        row_exchange(lambda q: tgs.at[q], tgc.at[j], S_TG)
        if far > 2:
            rs_step(3)
        grad_chunk(y)

        got(S_LRZ)
        lrs[...] = (2.0 * sum_of(lrz, nz)).astype(BF)
        row_exchange(lambda q: lrs, lrt.at[:, col(j)], S_LRR)
        for s in range(4, far + 1):
            rs_step(s)

        got(S_LRR)
        of = slw[0:1, :]
        lr = lrt[...].astype(F32)
        for yy in range(ny):
            mbig[yy * R : (yy + 1) * R, :] = jnp.where(of == slot_id(j, yy), lr, 0.0).astype(BF)
        pbs[...] = (
            jnp.dot(mbig[: ny * R, :], dyr[...].reshape(rw * T, C), preferred_element_type=F32)
            .astype(BF)
            .reshape(ny, R, C)
        )
        y_exchange(lambda q: pbs.at[q], gbp.at[y], S_GB)
        doubled(lrt)
        spread([slot_id(j, yy) for yy in range(ny)])
        vcs[...] = (
            jnp.dot(mt[:, : ny * R], ug[...].reshape(ny * R, C), preferred_element_type=F32)
            .astype(BF)
            .reshape(rw, T, C)
        )
        row_exchange(lambda q: vcs.at[q], vc.at[j], S_VC)

        for h in range(2):
            total = pa[y, hrows(h)]
            for d in range(2):
                n = ring_steps(ny, d, h)
                if n > 0:
                    rs_got(d, h, n)
                    total = total + rb[d, h, n - 1].astype(F32)
            for k in range(hw):
                fin[h * hw + k] = total[k * R : (k + 1) * R].astype(BF)
        row_exchange(lambda q: fin.at[q], gar.at[j], S_GA)

        got(S_TG)
        for k in range(rw):
            cols = slice(k * C, (k + 1) * C)
            tg_out[:, cols] = (fz[:, cols] + tgc[k].astype(F32)).astype(BF)
        got(S_BZ)
        got(S_VC)
        v_out[...] = (sum_of(bz, nz) + sum_of(vc, rw)).astype(BF)
        got(S_GB)
        gb_out[...] = sum_of(gbp, ny)
        got(S_GA)
        for k in range(rw):
            ga_out[:, k * C : (k + 1) * C] = gar[k].astype(F32)

    work()

    for one in started:
        if isinstance(one, tuple):
            if one not in done:
                one[0](*one[1:]).wait_recv()
            one[0](*one[1:]).wait_send()
        else:
            if one not in done:
                got(one)
            ref = arrives[one][1]
            pltpu.make_async_copy(ref, ref, ss.at[one]).wait()


def hand_over(*refs):
    sems = refs[8]
    copies = [pltpu.make_async_copy(refs[i], refs[4 + i], sems.at[i]) for i in range(4)]
    for copy in copies:
        copy.start()
    for copy in copies:
        copy.wait()


def shards(nx, ny, nz, tokens, weight, down, up, dy, adapter, lengths, table):
    rw = 2 * nx
    f = rw * C
    steps = max(1, ny // 2)
    hr = rw // 2 * R
    vm = pltpu.VMEM
    anywhere = pl.BlockSpec(memory_space=pl.ANY)
    vmem = pl.BlockSpec(memory_space=pltpu.VMEM)
    smem = pl.BlockSpec(memory_space=pltpu.SMEM)
    outs = (
        jax.ShapeDtypeStruct((T, C), BF),
        jax.ShapeDtypeStruct((T, f), BF),
        jax.ShapeDtypeStruct((R, f), F32),
        jax.ShapeDtypeStruct((R, C), F32),
    )
    made = pl.pallas_call(
        functools.partial(kernel, nx, ny, nz),
        out_shape=outs,
        in_specs=[anywhere] * 5 + [smem] * 3,
        out_specs=(vmem, vmem, vmem, vmem),
        scratch_shapes=[
            vm((T, f), BF),
            vm((f, nz * C), BF),
            vm((rw, T, C), BF),
            vm((ny, rw, R, C), BF),
            vm((rw, T, C), BF),
            vm((8, rw * T), jnp.int32),
            vm((8, T), jnp.int32),
            vm((T, nz * C), BF),
            vm((ny, R, C), BF),
            vm((rw, R, T), BF),
            vm((rw, R, T), BF),
            vm((R, T), BF),
            vm((nz, R, T), BF),
            vm((R, T), BF),
            vm((R, rw * T), BF),
            vm((nz, T, C), BF),
            vm((nz, T, C), BF),
            vm((T, f), F32),
            vm((rw, R, T), F32),
            vm((rw, R, T), BF),
            vm((rw, R, T), BF),
            vm((R, T), BF),
            vm((nz, R, T), BF),
            vm((R, T), BF),
            vm((R, rw * T), BF),
            vm((max(rw, ny) * R, rw * T), BF),
            vm((rw * T, max(rw, ny) * R), BF),
            vm((rw * T, 128), F32),
            vm((rw * T, 128), F32),
            vm((rw * T, C), F32),
            vm((rw, T, C), BF),
            vm((rw, T, C), BF),
            vm((rw, T, C), BF),
            vm((rw, T, C), BF),
            vm((ny, R, C), BF),
            vm((ny, R, C), BF),
            vm((ny, rw * R, C), F32),
            vm((ny, rw * R, C), BF),
            vm((2, 2, steps, hr, C), BF),
            vm((rw, R, C), BF),
            vm((rw, R, C), BF),
            pltpu.SemaphoreType.DMA((N_STAGES,)),
            pltpu.SemaphoreType.DMA((N_STAGES,)),
            pltpu.SemaphoreType.DMA((2, 2, steps)),
            pltpu.SemaphoreType.DMA((2, 2, steps)),
            pltpu.SemaphoreType.DMA((2, 2, steps)),
            pltpu.SemaphoreType.DMA((2, 2, steps)),
            pltpu.SemaphoreType.DMA((2,)),
        ],
        compiler_params=pltpu.CompilerParams(
            collective_id=0, has_side_effects=True, vmem_limit_bytes=LIMIT
        ),
    )(
        tokens,
        weight,
        jnp.swapaxes(down[0], 0, 1),
        up[0],
        dy,
        adapter.reshape(-1),
        lengths.reshape(-1),
        table,
    )
    values, token_grad, grad_a, grad_b = pl.pallas_call(
        hand_over,
        out_shape=outs,
        in_specs=[anywhere] * 4,
        out_specs=(anywhere,) * 4,
        scratch_shapes=[pltpu.SemaphoreType.DMA((4,))],
    )(*made)
    return values, token_grad, jnp.swapaxes(grad_a, 0, 1)[None], grad_b[None]


def solution(mesh, nx=4):
    dp, nz = mesh.shape["dp"], mesh.shape["tensor"]
    return jax.shard_map(
        functools.partial(shards, nx, dp // (2 * nx), nz),
        mesh=mesh,
        in_specs=(
            P("dp", "tensor"),
            P("tensor", None),
            P("dp", "tensor", None),
            P("dp", None, "tensor"),
            P("dp", "tensor"),
            P("dp", None),
            P("dp", None),
            P(),
        ),
        out_specs=(
            P("dp", "tensor"),
            P("dp", "tensor"),
            P("dp", "tensor", None),
            P("dp", None, "tensor"),
        ),
        check_vma=False,
    )
```

```python
import functools

import jax
import jax.numpy as jnp
from jax import lax
from jax.experimental import pallas as pl
from jax.experimental.pallas import tpu as pltpu
from jax.sharding import PartitionSpec as P

LIMIT = 56 * 1024 * 1024
MESH = pl.DeviceIdType.MESH
BF = jnp.bfloat16
F32 = jnp.float32
NT = (((1,), (1,)), ((), ()))
T = 128
R = 64
C = 128

(S_DT, S_DY, S_SL, S_X, S_DYZ, S_U, S_LGP, S_LGZ, S_LGR, S_BZ, S_LRP, S_LRZ, S_LRR, S_TG, S_VC, S_GB, S_GA) = range(17)
N_STAGES = 17


def ring_steps(ny, d, h):
    return ny // 2 if d == h else ny - 1 - ny // 2


def kernel(
    nx, ny, nz,
    x_hbm, w_hbm, dt_hbm, u_hbm, dy_hbm, adp, lens, tab,
    v_out, tg_out, ga_out, gb_out,
    xv, wv, xr, dg, dyr, slw, slo, dyf, ug,
    lgps, lgp, lgzs, lgz, lgs, lgt,
    bs, bz, fz,
    lracc, lrps, lrp, lrzs, lrz, lrs, lrt,
    mbig, mt, two, st, tgacc, tgs, tgc, vcs, vc, pbs, gbp,
    pa, pas, rb, fin, gar,
    ss, rs, ag_s, ag_r, rs_s, rs_r, ld,
):
    rw = 2 * nx
    hw = rw // 2
    me = lax.axis_index("dp")
    z = lax.axis_index("tensor")
    c = me % 2
    y = (me // 2) % ny
    x = me // (2 * ny)
    j = x * 2 + c

    def row_dev(jj):
        odd = lax.rem(jj, 2)
        return ny * (jj - odd) + odd + 2 * y

    def y_dev(yy):
        return x * (2 * ny) + yy * 2 + c

    def slot_id(jj, yy):
        return (jj // 2) * (2 * ny) + yy * 2 + jj % 2

    def col(i):
        return pl.ds(pl.multiple_of(i * 128, 128), 128)

    row = pl.ds(0, rw - 1)
    row_cols = pl.ds(0, (rw - 1) * 128)
    zs = pl.ds(0, nz - 1)
    ys = pl.ds(0, ny - 1)
    arrives = {
        S_DT: (dg.at[y], dg.at[0, row]),
        S_DY: (dyr, dyr.at[row]),
        S_SL: (slw, slw.at[:, row_cols]),
        S_X: (xr, xr.at[row]),
        S_DYZ: (dyf, dyf.at[:, pl.ds(0, (nz - 1) * 128)]),
        S_U: (ug, ug.at[ys]),
        S_LGP: (lgp, lgp.at[row]),
        S_LGZ: (lgz, lgz.at[zs]),
        S_LGR: (lgt, lgt.at[:, row_cols]),
        S_BZ: (bz, bz.at[zs]),
        S_LRP: (lrp, lrp.at[row]),
        S_LRZ: (lrz, lrz.at[zs]),
        S_LRR: (lrt, lrt.at[:, row_cols]),
        S_TG: (tgc, tgc.at[row]),
        S_VC: (vc, vc.at[row]),
        S_GB: (gbp, gbp.at[ys]),
        S_GA: (gar, fin.at[row]),
    }
    started, done = [], []

    def rcopy(src, dst, s, r, dev):
        return pltpu.make_async_remote_copy(
            src_ref=src, dst_ref=dst, send_sem=s, recv_sem=r, device_id=dev, device_id_type=MESH
        )

    def exchange(n, mine, dev, src, dst, stage):
        @pl.loop(1, n)
        def _(i):
            q = lax.rem(mine + i, n)
            rcopy(src(q), dst, ss.at[stage], rs.at[stage], dev(q)).start()

        pltpu.make_async_copy(src(mine), dst, rs.at[stage]).start()
        started.append(stage)

    def row_exchange(src, dst, stage):
        exchange(rw, j, lambda q: (row_dev(q), z), src, dst, stage)

    def y_exchange(src, dst, stage):
        exchange(ny, y, lambda q: (y_dev(q), z), src, dst, stage)

    def z_exchange(src, dst, stage):
        exchange(nz, z, lambda q: (me, q), src, dst, stage)

    def got(stage):
        ref = arrives[stage][0]
        pltpu.make_async_copy(ref, ref, rs.at[stage]).wait()
        done.append(stage)

    barrier = pltpu.get_barrier_semaphore()

    @pl.loop(1, rw)
    def _(i):
        pl.semaphore_signal(barrier, inc=1, device_id=(row_dev((j + i) % rw), z), device_id_type=MESH)

    @pl.loop(1, ny)
    def _(i):
        pl.semaphore_signal(barrier, inc=1, device_id=(y_dev((y + i) % ny), z), device_id_type=MESH)

    @pl.loop(1, nz)
    def _(i):
        pl.semaphore_signal(barrier, inc=1, device_id=(me, (z + i) % nz), device_id_type=MESH)

    load_w = pltpu.make_async_copy(w_hbm, wv, ld.at[0])
    load_x = pltpu.make_async_copy(x_hbm, xv, ld.at[1])
    load_x.start()
    load_w.start()

    position = lax.broadcasted_iota(jnp.int32, (8, T), 1)
    slots = jnp.full((8, T), 0, jnp.int32)
    begin = jnp.int32(0)
    for k in range(8):
        slots = jnp.where(position >= begin, tab[adp[k]], slots)
        begin = begin + lens[k]
    slo[...] = slots

    def work():
        pl.semaphore_wait(barrier, rw + ny + nz - 3)

        row_exchange(lambda q: dt_hbm.at[:, col(q)], dg.at[y, j], S_DT)
        y_exchange(lambda q: u_hbm, ug.at[y], S_U)
        row_exchange(lambda q: slo, slw.at[:, col(j)], S_SL)
        row_exchange(lambda q: dy_hbm, dyr.at[j], S_DY)
        z_exchange(lambda q: dy_hbm, dyf.at[:, col(z)], S_DYZ)
        row_exchange(lambda q: x_hbm.at[:, col(q)], xr.at[j], S_X)

        def half(h):
            return pl.ds(h * hw, hw)

        def ag_copy(d, h, s):
            yy = (y - (s - 1) if d == 0 else y + (s - 1)) % ny
            to = (y + 1 if d == 0 else y - 1) % ny
            block = dg.at[yy, half(h)]
            return rcopy(block, block, ag_s.at[d, h, s - 1], ag_r.at[d, h, s - 1], (y_dev(to), z))

        def ag_send(s):
            for h in range(2):
                for d in range(2):
                    if s <= ring_steps(ny, d, h):
                        started.append((ag_copy, d, h, s))
                        ag_copy(d, h, s).start()

        def ag_got(s):
            for h in range(2):
                for d in range(2):
                    if s <= ring_steps(ny, d, h):
                        ag_copy(d, h, s).wait_recv()
                        done.append((ag_copy, d, h, s))
                        if s + 1 <= ring_steps(ny, d, h):
                            started.append((ag_copy, d, h, s + 1))
                            ag_copy(d, h, s + 1).start()

        def sum_of(ref, n):
            total = ref[0].astype(F32)
            for i in range(1, n):
                total = total + ref[i].astype(F32)
            return total

        def low_rank_chunk(yy):
            panels = dg[yy].reshape(rw * R, C)

            @pl.loop(0, rw // 2)
            def _(i):
                pair = xr[pl.ds(2 * i, 2)].reshape(2 * T, C)
                wide = lax.dot_general(panels, pair, NT, preferred_element_type=F32)
                for e in range(2):
                    of = slw[0:1, col(2 * i + e)]
                    total = lracc[2 * i + e]
                    for k in range(rw):
                        total = total + jnp.where(
                            of == slot_id(k, yy), wide[k * R : (k + 1) * R, e * T : (e + 1) * T], 0.0
                        )
                    lracc[2 * i + e] = total

        def grad_chunk(yy):
            of = slw[0:1, :]
            lg = lgt[...].astype(F32)
            for k in range(rw):
                mbig[k * R : (k + 1) * R, :] = jnp.where(of == slot_id(k, yy), lg, 0.0).astype(BF)
            pa[yy] = jnp.dot(mbig[: rw * R, :], xr[...].reshape(rw * T, C), preferred_element_type=F32)

        def hrows(h):
            return pl.ds(h * hw * R, hw * R)

        def rs_copy(d, h, s):
            n = ring_steps(ny, d, h)
            dest = (y + (n - s + 1) if d == 0 else y - (n - s + 1)) % ny
            to = (y + 1 if d == 0 else y - 1) % ny
            return rcopy(
                pas.at[dest, hrows(h)], rb.at[d, h, s - 1], rs_s.at[d, h, s - 1], rs_r.at[d, h, s - 1], (y_dev(to), z)
            )

        def rs_send(d, h, s):
            n = ring_steps(ny, d, h)
            if s > n:
                return
            dest = (y + (n - s + 1) if d == 0 else y - (n - s + 1)) % ny
            part = pa[dest, hrows(h)]
            if s > 1:
                rs_got(d, h, s - 1)
                part = part + rb[d, h, s - 2].astype(F32)
            pas[dest, hrows(h)] = part.astype(BF)
            started.append((rs_copy, d, h, s))
            rs_copy(d, h, s).start()

        def rs_got(d, h, s):
            rs_copy(d, h, s).wait_recv()
            done.append((rs_copy, d, h, s))

        far = ny // 2

        def rs_step(s):
            for d in range(2):
                rs_send(d, d, s)
            for d in range(2):
                rs_send(d, 1 - d, s)

        def both(step, distance):
            step((y + distance) % ny)
            step((y - distance) % ny)

        lane = lax.broadcasted_iota(jnp.int32, (T, 128), 1)

        def rows_of(b):
            return pl.ds(pl.multiple_of(b * T, T), T)

        def doubled(src):
            @pl.loop(0, rw)
            def _(b):
                one = src[:, col(b)].astype(F32)
                two[rows_of(b), :] = jnp.concatenate([one, one], axis=0).T

        def spread(ids):
            @pl.loop(0, rw)
            def _(b):
                of = st[rows_of(b), :]
                rows = two[rows_of(b), :]
                for m in range(len(ids) // 2):
                    want = jnp.where(lane < R, ids[2 * m], ids[2 * m + 1]).astype(F32)
                    mt[rows_of(b), m * 128 : (m + 1) * 128] = jnp.where(of == want, rows, 0.0).astype(BF)

        load_x.wait()
        load_w.wait()

        @pl.loop(0, nz // 2)
        def _(i):
            part = jnp.dot(
                xv[...], wv[:, pl.ds(pl.multiple_of(i * 256, 256), 256)], preferred_element_type=F32
            ).astype(BF)
            bs[2 * i] = part[:, :C]
            bs[2 * i + 1] = part[:, C:]

        got(S_DT)
        ag_send(1)

        got(S_U)
        got(S_SL)
        got(S_DY)

        @pl.loop(0, rw)
        def _(b):
            wide = lax.dot_general(
                ug[...].reshape(ny * R, C), dyr[b], NT, preferred_element_type=F32
            )
            of = slw[0:1, col(b)]
            total = jnp.zeros((R, T), F32)
            for yy in range(ny):
                total = total + jnp.where(of == slot_id(j, yy), wide[yy * R : (yy + 1) * R], 0.0)
            lgps[b] = total.astype(BF)

        row_exchange(lambda q: lgps.at[q], lgp.at[j], S_LGP)

        @pl.loop(0, rw)
        def _(b):
            of = jnp.broadcast_to(slw[0:1, col(b)].astype(F32), (T, T))
            st[pl.ds(pl.multiple_of(b * T, T), T), :] = of.T
            lracc[b] = jnp.zeros((R, T), F32)

        ag_got(1)
        got(S_LGP)
        lgzs[...] = sum_of(lgp, rw).astype(BF)
        z_exchange(lambda q: lgzs, lgz.at[z], S_LGZ)

        got(S_X)
        low_rank_chunk(y)
        if far > 1:
            ag_got(2)
            both(low_rank_chunk, 1)

        got(S_DYZ)

        @pl.loop(0, rw // 2)
        def _(i):
            f = pl.ds(pl.multiple_of(i * 256, 256), 256)
            fz[:, f] = lax.dot_general(dyf[...], wv[f, :], NT, preferred_element_type=F32)

        if far > 2:
            ag_got(3)
        if far > 2:
            both(low_rank_chunk, 2)

        got(S_LGZ)
        lgs[...] = (2.0 * sum_of(lgz, nz)).astype(BF)
        row_exchange(lambda q: lgs, lgt.at[:, col(j)], S_LGR)

        for s in range(4, far + 1):
            ag_got(s)
        for s in range(3, far):
            both(low_rank_chunk, s)
        low_rank_chunk((y + far) % ny)

        @pl.loop(0, rw)
        def _(b):
            lrps[b] = lracc[b].astype(BF)

        row_exchange(lambda q: lrps.at[q], lrp.at[j], S_LRP)

        got(S_LGR)
        grad_chunk((y + far) % ny)
        for d in range(2):
            rs_send(d, d, 1)
        if far > 1:
            both(grad_chunk, far - 1)
            for d in range(2):
                rs_send(d, 1 - d, 1)

        got(S_LRP)
        lrzs[...] = sum_of(lrp, rw).astype(BF)
        z_exchange(lambda q: lrzs, lrz.at[z], S_LRZ)
        z_exchange(lambda q: bs.at[q], bz.at[z], S_BZ)

        for s in range(2, far):
            both(grad_chunk, far - s)
        if far > 1:
            rs_step(2)
        doubled(lgt)
        tgacc[...] = jnp.zeros_like(tgacc)

        @pl.loop(0, ny)
        def _(yy):
            spread([slot_id(k, yy) for k in range(rw)])
            tgacc[...] += jnp.dot(
                mt[:, : rw * R], dg[yy].reshape(rw * R, C), preferred_element_type=F32
            )

        tgs[...] = tgacc[...].astype(BF).reshape(rw, T, C)
        row_exchange(lambda q: tgs.at[q], tgc.at[j], S_TG)
        if far > 2:
            rs_step(3)
        grad_chunk(y)

        got(S_LRZ)
        lrs[...] = (2.0 * sum_of(lrz, nz)).astype(BF)
        row_exchange(lambda q: lrs, lrt.at[:, col(j)], S_LRR)
        for s in range(4, far + 1):
            rs_step(s)

        got(S_LRR)
        of = slw[0:1, :]
        lr = lrt[...].astype(F32)
        for yy in range(ny):
            mbig[yy * R : (yy + 1) * R, :] = jnp.where(of == slot_id(j, yy), lr, 0.0).astype(BF)
        pbs[...] = (
            jnp.dot(mbig[: ny * R, :], dyr[...].reshape(rw * T, C), preferred_element_type=F32)
            .astype(BF)
            .reshape(ny, R, C)
        )
        y_exchange(lambda q: pbs.at[q], gbp.at[y], S_GB)
        doubled(lrt)
        spread([slot_id(j, yy) for yy in range(ny)])
        vcs[...] = (
            jnp.dot(mt[:, : ny * R], ug[...].reshape(ny * R, C), preferred_element_type=F32)
            .astype(BF)
            .reshape(rw, T, C)
        )
        row_exchange(lambda q: vcs.at[q], vc.at[j], S_VC)

        for h in range(2):
            total = pa[y, hrows(h)]
            for d in range(2):
                n = ring_steps(ny, d, h)
                if n > 0:
                    rs_got(d, h, n)
                    total = total + rb[d, h, n - 1].astype(F32)
            for k in range(hw):
                fin[h * hw + k] = total[k * R : (k + 1) * R].astype(BF)
        row_exchange(lambda q: fin.at[q], gar.at[j], S_GA)

        got(S_TG)
        for k in range(rw):
            cols = slice(k * C, (k + 1) * C)
            tg_out[:, cols] = (fz[:, cols] + tgc[k].astype(F32)).astype(BF)
        got(S_BZ)
        got(S_VC)
        v_out[...] = (sum_of(bz, nz) + sum_of(vc, rw)).astype(BF)
        got(S_GB)
        gb_out[...] = sum_of(gbp, ny)
        got(S_GA)
        for k in range(rw):
            ga_out[:, k * C : (k + 1) * C] = gar[k].astype(F32)

    work()

    for one in started:
        if isinstance(one, tuple):
            if one not in done:
                one[0](*one[1:]).wait_recv()
            one[0](*one[1:]).wait_send()
        else:
            if one not in done:
                got(one)
            ref = arrives[one][1]
            pltpu.make_async_copy(ref, ref, ss.at[one]).wait()


def hand_over(*refs):
    sems = refs[8]
    copies = [pltpu.make_async_copy(refs[i], refs[4 + i], sems.at[i]) for i in range(4)]
    for copy in copies:
        copy.start()
    for copy in copies:
        copy.wait()


def shards(nx, ny, nz, tokens, weight, down, up, dy, adapter, lengths, table):
    rw = 2 * nx
    f = rw * C
    steps = max(1, ny // 2)
    hr = rw // 2 * R
    vm = pltpu.VMEM
    anywhere = pl.BlockSpec(memory_space=pl.ANY)
    vmem = pl.BlockSpec(memory_space=pltpu.VMEM)
    smem = pl.BlockSpec(memory_space=pltpu.SMEM)
    outs = (
        jax.ShapeDtypeStruct((T, C), BF),
        jax.ShapeDtypeStruct((T, f), BF),
        jax.ShapeDtypeStruct((R, f), F32),
        jax.ShapeDtypeStruct((R, C), F32),
    )
    kept = tuple(pltpu.VMEM(o.shape, o.dtype) for o in outs)
    made = pl.pallas_call(
        functools.partial(kernel, nx, ny, nz),
        out_shape=kept,
        in_specs=[anywhere] * 5 + [smem] * 3,
        out_specs=(vmem, vmem, vmem, vmem),
        scratch_shapes=[
            vm((T, f), BF),
            vm((f, nz * C), BF),
            vm((rw, T, C), BF),
            vm((ny, rw, R, C), BF),
            vm((rw, T, C), BF),
            vm((8, rw * T), jnp.int32),
            vm((8, T), jnp.int32),
            vm((T, nz * C), BF),
            vm((ny, R, C), BF),
            vm((rw, R, T), BF),
            vm((rw, R, T), BF),
            vm((R, T), BF),
            vm((nz, R, T), BF),
            vm((R, T), BF),
            vm((R, rw * T), BF),
            vm((nz, T, C), BF),
            vm((nz, T, C), BF),
            vm((T, f), F32),
            vm((rw, R, T), F32),
            vm((rw, R, T), BF),
            vm((rw, R, T), BF),
            vm((R, T), BF),
            vm((nz, R, T), BF),
            vm((R, T), BF),
            vm((R, rw * T), BF),
            vm((max(rw, ny) * R, rw * T), BF),
            vm((rw * T, max(rw, ny) * R), BF),
            vm((rw * T, 128), F32),
            vm((rw * T, 128), F32),
            vm((rw * T, C), F32),
            vm((rw, T, C), BF),
            vm((rw, T, C), BF),
            vm((rw, T, C), BF),
            vm((rw, T, C), BF),
            vm((ny, R, C), BF),
            vm((ny, R, C), BF),
            vm((ny, rw * R, C), F32),
            vm((ny, rw * R, C), BF),
            vm((2, 2, steps, hr, C), BF),
            vm((rw, R, C), BF),
            vm((rw, R, C), BF),
            pltpu.SemaphoreType.DMA((N_STAGES,)),
            pltpu.SemaphoreType.DMA((N_STAGES,)),
            pltpu.SemaphoreType.DMA((2, 2, steps)),
            pltpu.SemaphoreType.DMA((2, 2, steps)),
            pltpu.SemaphoreType.DMA((2, 2, steps)),
            pltpu.SemaphoreType.DMA((2, 2, steps)),
            pltpu.SemaphoreType.DMA((2,)),
        ],
        compiler_params=pltpu.CompilerParams(
            collective_id=0, has_side_effects=True, vmem_limit_bytes=LIMIT
        ),
    )(
        tokens,
        weight,
        jnp.swapaxes(down[0], 0, 1),
        up[0],
        dy,
        adapter.reshape(-1),
        lengths.reshape(-1),
        table,
    )
    values, token_grad, grad_a, grad_b = pl.pallas_call(
        hand_over,
        out_shape=outs,
        in_specs=[anywhere] * 4,
        out_specs=(anywhere,) * 4,
        scratch_shapes=[pltpu.SemaphoreType.DMA((4,))],
    )(*[pltpu.with_memory_space_constraint(one, pltpu.VMEM) for one in made])
    return values, token_grad, jnp.swapaxes(grad_a, 0, 1)[None], grad_b[None]


def solution(mesh, nx=4):
    dp, nz = mesh.shape["dp"], mesh.shape["tensor"]
    return jax.shard_map(
        functools.partial(shards, nx, dp // (2 * nx), nz),
        mesh=mesh,
        in_specs=(
            P("dp", "tensor"),
            P("tensor", None),
            P("dp", "tensor", None),
            P("dp", None, "tensor"),
            P("dp", "tensor"),
            P("dp", None),
            P("dp", None),
            P(),
        ),
        out_specs=(
            P("dp", "tensor"),
            P("dp", "tensor"),
            P("dp", "tensor", None),
            P("dp", None, "tensor"),
        ),
        check_vma=False,
    )
```

```python
import functools

import jax
import jax.numpy as jnp
from jax import lax
from jax.experimental import pallas as pl
from jax.experimental.pallas import tpu as pltpu
from jax.sharding import PartitionSpec as P

LIMIT = 56 * 1024 * 1024
MESH = pl.DeviceIdType.MESH
BF = jnp.bfloat16
F32 = jnp.float32
NT = (((1,), (1,)), ((), ()))
T = 128
R = 64
C = 128

(S_DT, S_DY, S_SL, S_X, S_DYZ, S_U, S_LGP, S_LGZ, S_LGR, S_BZ, S_LRP, S_LRZ, S_LRR, S_TG, S_VC, S_GB, S_GA) = range(17)
N_STAGES = 17


def ring_steps(ny, d, h):
    return ny // 2 if d == h else ny - 1 - ny // 2


def kernel(
    nx, ny, nz,
    x_hbm, w_hbm, dt_hbm, u_hbm, dy_hbm, adp, lens, tab,
    v_out, tg_out, ga_out, gb_out,
    xv, wv, xr, dg, dyr, slw, slo, dyf, ug,
    lgps, lgp, lgzs, lgz, lgs, lgt,
    bs, bz, fz,
    lracc, lrps, lrp, lrzs, lrz, lrs, lrt,
    mbig, mt, two, st, tgacc, tgs, tgc, vcs, vc, pbs, gbp,
    pa, pas, rb, fin, gar,
    ss, rs, ag_s, ag_r, rs_s, rs_r, ld,
):
    rw = 2 * nx
    hw = rw // 2
    me = lax.axis_index("dp")
    z = lax.axis_index("tensor")
    c = me % 2
    y = (me // 2) % ny
    x = me // (2 * ny)
    j = x * 2 + c

    def row_dev(jj):
        odd = lax.rem(jj, 2)
        return ny * (jj - odd) + odd + 2 * y

    def y_dev(yy):
        return x * (2 * ny) + yy * 2 + c

    def slot_id(jj, yy):
        return (jj // 2) * (2 * ny) + yy * 2 + jj % 2

    def col(i):
        return pl.ds(pl.multiple_of(i * 128, 128), 128)

    row = pl.ds(0, rw - 1)
    row_cols = pl.ds(0, (rw - 1) * 128)
    zs = pl.ds(0, nz - 1)
    ys = pl.ds(0, ny - 1)
    arrives = {
        S_DT: (dg.at[y], dg.at[0, row]),
        S_DY: (dyr, dyr.at[row]),
        S_SL: (slw, slw.at[:, row_cols]),
        S_X: (xr, xr.at[row]),
        S_DYZ: (dyf, dyf.at[:, pl.ds(0, (nz - 1) * 128)]),
        S_U: (ug, ug.at[ys]),
        S_LGP: (lgp, lgp.at[row]),
        S_LGZ: (lgz, lgz.at[zs]),
        S_LGR: (lgt, lgt.at[:, row_cols]),
        S_BZ: (bz, bz.at[zs]),
        S_LRP: (lrp, lrp.at[row]),
        S_LRZ: (lrz, lrz.at[zs]),
        S_LRR: (lrt, lrt.at[:, row_cols]),
        S_TG: (tgc, tgc.at[row]),
        S_VC: (vc, vc.at[row]),
        S_GB: (gbp, gbp.at[ys]),
        S_GA: (gar, fin.at[row]),
    }
    started, done = [], []

    def rcopy(src, dst, s, r, dev):
        return pltpu.make_async_remote_copy(
            src_ref=src, dst_ref=dst, send_sem=s, recv_sem=r, device_id=dev, device_id_type=MESH
        )

    def partners(n, mine, dev):
        order = sorted(range(1, n), key=lambda i: (-min(i, n - i), i))
        return [(q, dev(q)) for q in [lax.rem(mine + i, n) for i in order]]

    row_peers = partners(rw, j, lambda q: (row_dev(q), z))
    y_peers = partners(ny, y, lambda q: (y_dev(q), z))
    z_peers = partners(nz, z, lambda q: (me, q))

    def exchange(peers, mine, src, dst, stage):
        for q, dev in peers:
            rcopy(src(q), dst, ss.at[stage], rs.at[stage], dev).start()
        pltpu.make_async_copy(src(mine), dst, rs.at[stage]).start()
        started.append(stage)

    def row_exchange(src, dst, stage):
        exchange(row_peers, j, src, dst, stage)

    def y_exchange(src, dst, stage):
        exchange(y_peers, y, src, dst, stage)

    def z_exchange(src, dst, stage):
        exchange(z_peers, z, src, dst, stage)

    def got(stage):
        ref = arrives[stage][0]
        pltpu.make_async_copy(ref, ref, rs.at[stage]).wait()
        done.append(stage)

    barrier = pltpu.get_barrier_semaphore()

    @pl.loop(1, rw)
    def _(i):
        pl.semaphore_signal(barrier, inc=1, device_id=(row_dev((j + i) % rw), z), device_id_type=MESH)

    @pl.loop(1, ny)
    def _(i):
        pl.semaphore_signal(barrier, inc=1, device_id=(y_dev((y + i) % ny), z), device_id_type=MESH)

    @pl.loop(1, nz)
    def _(i):
        pl.semaphore_signal(barrier, inc=1, device_id=(me, (z + i) % nz), device_id_type=MESH)

    load_w = pltpu.make_async_copy(w_hbm, wv, ld.at[0])
    load_x = pltpu.make_async_copy(x_hbm, xv, ld.at[1])
    load_x.start()
    load_w.start()

    position = lax.broadcasted_iota(jnp.int32, (8, T), 1)
    slots = jnp.full((8, T), 0, jnp.int32)
    begin = jnp.int32(0)
    for k in range(8):
        slots = jnp.where(position >= begin, tab[adp[k]], slots)
        begin = begin + lens[k]
    slo[...] = slots

    def work():
        pl.semaphore_wait(barrier, rw + ny + nz - 3)

        row_exchange(lambda q: dt_hbm.at[:, col(q)], dg.at[y, j], S_DT)
        y_exchange(lambda q: u_hbm, ug.at[y], S_U)
        row_exchange(lambda q: slo, slw.at[:, col(j)], S_SL)
        row_exchange(lambda q: dy_hbm, dyr.at[j], S_DY)
        z_exchange(lambda q: dy_hbm, dyf.at[:, col(z)], S_DYZ)
        row_exchange(lambda q: x_hbm.at[:, col(q)], xr.at[j], S_X)

        def half(h):
            return pl.ds(h * hw, hw)

        def ag_copy(d, h, s):
            yy = (y - (s - 1) if d == 0 else y + (s - 1)) % ny
            to = (y + 1 if d == 0 else y - 1) % ny
            block = dg.at[yy, half(h)]
            return rcopy(block, block, ag_s.at[d, h, s - 1], ag_r.at[d, h, s - 1], (y_dev(to), z))

        def ag_send(s):
            for h in range(2):
                for d in range(2):
                    if s <= ring_steps(ny, d, h):
                        started.append((ag_copy, d, h, s))
                        ag_copy(d, h, s).start()

        def ag_got(s):
            for h in range(2):
                for d in range(2):
                    if s <= ring_steps(ny, d, h):
                        ag_copy(d, h, s).wait_recv()
                        done.append((ag_copy, d, h, s))
                        if s + 1 <= ring_steps(ny, d, h):
                            started.append((ag_copy, d, h, s + 1))
                            ag_copy(d, h, s + 1).start()

        def sum_of(ref, n):
            total = ref[0].astype(F32)
            for i in range(1, n):
                total = total + ref[i].astype(F32)
            return total

        def low_rank_chunk(yy):
            panels = dg[yy].reshape(rw * R, C)

            @pl.loop(0, rw // 2)
            def _(i):
                pair = xr[pl.ds(2 * i, 2)].reshape(2 * T, C)
                wide = lax.dot_general(panels, pair, NT, preferred_element_type=F32)
                for e in range(2):
                    of = slw[0:1, col(2 * i + e)]
                    total = lracc[2 * i + e]
                    for k in range(rw):
                        total = total + jnp.where(
                            of == slot_id(k, yy), wide[k * R : (k + 1) * R, e * T : (e + 1) * T], 0.0
                        )
                    lracc[2 * i + e] = total

        def grad_chunk(yy):
            of = slw[0:1, :]
            lg = lgt[...].astype(F32)
            for k in range(rw):
                mbig[k * R : (k + 1) * R, :] = jnp.where(of == slot_id(k, yy), lg, 0.0).astype(BF)
            pa[yy] = jnp.dot(mbig[: rw * R, :], xr[...].reshape(rw * T, C), preferred_element_type=F32)

        def hrows(h):
            return pl.ds(h * hw * R, hw * R)

        def rs_copy(d, h, s):
            n = ring_steps(ny, d, h)
            dest = (y + (n - s + 1) if d == 0 else y - (n - s + 1)) % ny
            to = (y + 1 if d == 0 else y - 1) % ny
            return rcopy(
                pas.at[dest, hrows(h)], rb.at[d, h, s - 1], rs_s.at[d, h, s - 1], rs_r.at[d, h, s - 1], (y_dev(to), z)
            )

        def rs_send(d, h, s):
            n = ring_steps(ny, d, h)
            if s > n:
                return
            dest = (y + (n - s + 1) if d == 0 else y - (n - s + 1)) % ny
            part = pa[dest, hrows(h)]
            if s > 1:
                rs_got(d, h, s - 1)
                part = part + rb[d, h, s - 2].astype(F32)
            pas[dest, hrows(h)] = part.astype(BF)
            started.append((rs_copy, d, h, s))
            rs_copy(d, h, s).start()

        def rs_got(d, h, s):
            rs_copy(d, h, s).wait_recv()
            done.append((rs_copy, d, h, s))

        far = ny // 2

        def rs_step(s):
            for d in range(2):
                rs_send(d, d, s)
            for d in range(2):
                rs_send(d, 1 - d, s)

        def both(step, distance):
            step((y + distance) % ny)
            step((y - distance) % ny)

        lane = lax.broadcasted_iota(jnp.int32, (T, 128), 1)

        def rows_of(b):
            return pl.ds(pl.multiple_of(b * T, T), T)

        def doubled(src):
            @pl.loop(0, rw)
            def _(b):
                one = src[:, col(b)].astype(F32)
                two[rows_of(b), :] = jnp.concatenate([one, one], axis=0).T

        def spread(ids):
            @pl.loop(0, rw)
            def _(b):
                of = st[rows_of(b), :]
                rows = two[rows_of(b), :]
                for m in range(len(ids) // 2):
                    want = jnp.where(lane < R, ids[2 * m], ids[2 * m + 1]).astype(F32)
                    mt[rows_of(b), m * 128 : (m + 1) * 128] = jnp.where(of == want, rows, 0.0).astype(BF)

        load_x.wait()
        load_w.wait()

        @pl.loop(0, nz // 2)
        def _(i):
            part = jnp.dot(
                xv[...], wv[:, pl.ds(pl.multiple_of(i * 256, 256), 256)], preferred_element_type=F32
            ).astype(BF)
            bs[2 * i] = part[:, :C]
            bs[2 * i + 1] = part[:, C:]

        got(S_DT)
        ag_send(1)

        got(S_U)
        got(S_SL)
        got(S_DY)

        @pl.loop(0, rw)
        def _(b):
            wide = lax.dot_general(
                ug[...].reshape(ny * R, C), dyr[b], NT, preferred_element_type=F32
            )
            of = slw[0:1, col(b)]
            total = jnp.zeros((R, T), F32)
            for yy in range(ny):
                total = total + jnp.where(of == slot_id(j, yy), wide[yy * R : (yy + 1) * R], 0.0)
            lgps[b] = total.astype(BF)

        row_exchange(lambda q: lgps.at[q], lgp.at[j], S_LGP)

        @pl.loop(0, rw)
        def _(b):
            of = jnp.broadcast_to(slw[0:1, col(b)].astype(F32), (T, T))
            st[pl.ds(pl.multiple_of(b * T, T), T), :] = of.T
            lracc[b] = jnp.zeros((R, T), F32)

        ag_got(1)
        got(S_LGP)
        lgzs[...] = sum_of(lgp, rw).astype(BF)
        z_exchange(lambda q: lgzs, lgz.at[z], S_LGZ)

        got(S_X)
        low_rank_chunk(y)
        if far > 1:
            ag_got(2)
            both(low_rank_chunk, 1)

        got(S_DYZ)

        @pl.loop(0, rw // 2)
        def _(i):
            f = pl.ds(pl.multiple_of(i * 256, 256), 256)
            fz[:, f] = lax.dot_general(dyf[...], wv[f, :], NT, preferred_element_type=F32)

        if far > 2:
            ag_got(3)
        if far > 2:
            both(low_rank_chunk, 2)

        got(S_LGZ)
        lgs[...] = (2.0 * sum_of(lgz, nz)).astype(BF)
        row_exchange(lambda q: lgs, lgt.at[:, col(j)], S_LGR)

        for s in range(4, far + 1):
            ag_got(s)
        for s in range(3, far):
            both(low_rank_chunk, s)
        low_rank_chunk((y + far) % ny)

        @pl.loop(0, rw)
        def _(b):
            lrps[b] = lracc[b].astype(BF)

        row_exchange(lambda q: lrps.at[q], lrp.at[j], S_LRP)

        got(S_LGR)
        grad_chunk((y + far) % ny)
        for d in range(2):
            rs_send(d, d, 1)
        if far > 1:
            both(grad_chunk, far - 1)
            for d in range(2):
                rs_send(d, 1 - d, 1)

        got(S_LRP)
        lrzs[...] = sum_of(lrp, rw).astype(BF)
        z_exchange(lambda q: lrzs, lrz.at[z], S_LRZ)
        z_exchange(lambda q: bs.at[q], bz.at[z], S_BZ)

        for s in range(2, far):
            both(grad_chunk, far - s)
        if far > 1:
            rs_step(2)
        doubled(lgt)
        tgacc[...] = jnp.zeros_like(tgacc)

        @pl.loop(0, ny)
        def _(yy):
            spread([slot_id(k, yy) for k in range(rw)])
            tgacc[...] += jnp.dot(
                mt[:, : rw * R], dg[yy].reshape(rw * R, C), preferred_element_type=F32
            )

        tgs[...] = tgacc[...].astype(BF).reshape(rw, T, C)
        row_exchange(lambda q: tgs.at[q], tgc.at[j], S_TG)
        if far > 2:
            rs_step(3)
        grad_chunk(y)

        got(S_LRZ)
        lrs[...] = (2.0 * sum_of(lrz, nz)).astype(BF)
        row_exchange(lambda q: lrs, lrt.at[:, col(j)], S_LRR)
        for s in range(4, far + 1):
            rs_step(s)

        got(S_LRR)
        of = slw[0:1, :]
        lr = lrt[...].astype(F32)
        for yy in range(ny):
            mbig[yy * R : (yy + 1) * R, :] = jnp.where(of == slot_id(j, yy), lr, 0.0).astype(BF)
        pbs[...] = (
            jnp.dot(mbig[: ny * R, :], dyr[...].reshape(rw * T, C), preferred_element_type=F32)
            .astype(BF)
            .reshape(ny, R, C)
        )
        y_exchange(lambda q: pbs.at[q], gbp.at[y], S_GB)
        doubled(lrt)
        spread([slot_id(j, yy) for yy in range(ny)])
        vcs[...] = (
            jnp.dot(mt[:, : ny * R], ug[...].reshape(ny * R, C), preferred_element_type=F32)
            .astype(BF)
            .reshape(rw, T, C)
        )
        row_exchange(lambda q: vcs.at[q], vc.at[j], S_VC)

        for h in range(2):
            total = pa[y, hrows(h)]
            for d in range(2):
                n = ring_steps(ny, d, h)
                if n > 0:
                    rs_got(d, h, n)
                    total = total + rb[d, h, n - 1].astype(F32)
            for k in range(hw):
                fin[h * hw + k] = total[k * R : (k + 1) * R].astype(BF)
        row_exchange(lambda q: fin.at[q], gar.at[j], S_GA)

        got(S_TG)
        for k in range(rw):
            cols = slice(k * C, (k + 1) * C)
            tg_out[:, cols] = (fz[:, cols] + tgc[k].astype(F32)).astype(BF)
        got(S_BZ)
        got(S_VC)
        v_out[...] = (sum_of(bz, nz) + sum_of(vc, rw)).astype(BF)
        got(S_GB)
        gb_out[...] = sum_of(gbp, ny)
        got(S_GA)
        for k in range(rw):
            ga_out[:, k * C : (k + 1) * C] = gar[k].astype(F32)

    work()

    for one in started:
        if isinstance(one, tuple):
            if one not in done:
                one[0](*one[1:]).wait_recv()
            one[0](*one[1:]).wait_send()
        else:
            if one not in done:
                got(one)
            ref = arrives[one][1]
            pltpu.make_async_copy(ref, ref, ss.at[one]).wait()


def hand_over(*refs):
    sems = refs[8]
    copies = [pltpu.make_async_copy(refs[i], refs[4 + i], sems.at[i]) for i in range(4)]
    for copy in copies:
        copy.start()
    for copy in copies:
        copy.wait()


def shards(nx, ny, nz, tokens, weight, down, up, dy, adapter, lengths, table):
    rw = 2 * nx
    f = rw * C
    steps = max(1, ny // 2)
    hr = rw // 2 * R
    vm = pltpu.VMEM
    anywhere = pl.BlockSpec(memory_space=pl.ANY)
    vmem = pl.BlockSpec(memory_space=pltpu.VMEM)
    smem = pl.BlockSpec(memory_space=pltpu.SMEM)
    outs = (
        jax.ShapeDtypeStruct((T, C), BF),
        jax.ShapeDtypeStruct((T, f), BF),
        jax.ShapeDtypeStruct((R, f), F32),
        jax.ShapeDtypeStruct((R, C), F32),
    )
    kept = tuple(pltpu.VMEM(o.shape, o.dtype) for o in outs)
    made = pl.pallas_call(
        functools.partial(kernel, nx, ny, nz),
        out_shape=kept,
        in_specs=[anywhere] * 5 + [smem] * 3,
        out_specs=(vmem, vmem, vmem, vmem),
        scratch_shapes=[
            vm((T, f), BF),
            vm((f, nz * C), BF),
            vm((rw, T, C), BF),
            vm((ny, rw, R, C), BF),
            vm((rw, T, C), BF),
            vm((8, rw * T), jnp.int32),
            vm((8, T), jnp.int32),
            vm((T, nz * C), BF),
            vm((ny, R, C), BF),
            vm((rw, R, T), BF),
            vm((rw, R, T), BF),
            vm((R, T), BF),
            vm((nz, R, T), BF),
            vm((R, T), BF),
            vm((R, rw * T), BF),
            vm((nz, T, C), BF),
            vm((nz, T, C), BF),
            vm((T, f), F32),
            vm((rw, R, T), F32),
            vm((rw, R, T), BF),
            vm((rw, R, T), BF),
            vm((R, T), BF),
            vm((nz, R, T), BF),
            vm((R, T), BF),
            vm((R, rw * T), BF),
            vm((max(rw, ny) * R, rw * T), BF),
            vm((rw * T, max(rw, ny) * R), BF),
            vm((rw * T, 128), F32),
            vm((rw * T, 128), F32),
            vm((rw * T, C), F32),
            vm((rw, T, C), BF),
            vm((rw, T, C), BF),
            vm((rw, T, C), BF),
            vm((rw, T, C), BF),
            vm((ny, R, C), BF),
            vm((ny, R, C), BF),
            vm((ny, rw * R, C), F32),
            vm((ny, rw * R, C), BF),
            vm((2, 2, steps, hr, C), BF),
            vm((rw, R, C), BF),
            vm((rw, R, C), BF),
            pltpu.SemaphoreType.DMA((N_STAGES,)),
            pltpu.SemaphoreType.DMA((N_STAGES,)),
            pltpu.SemaphoreType.DMA((2, 2, steps)),
            pltpu.SemaphoreType.DMA((2, 2, steps)),
            pltpu.SemaphoreType.DMA((2, 2, steps)),
            pltpu.SemaphoreType.DMA((2, 2, steps)),
            pltpu.SemaphoreType.DMA((2,)),
        ],
        compiler_params=pltpu.CompilerParams(
            collective_id=0, has_side_effects=True, vmem_limit_bytes=LIMIT
        ),
    )(
        tokens,
        weight,
        jnp.swapaxes(down[0], 0, 1),
        up[0],
        dy,
        adapter.reshape(-1),
        lengths.reshape(-1),
        table,
    )
    values, token_grad, grad_a, grad_b = pl.pallas_call(
        hand_over,
        out_shape=outs,
        in_specs=[anywhere] * 4,
        out_specs=(anywhere,) * 4,
        scratch_shapes=[pltpu.SemaphoreType.DMA((4,))],
    )(*[pltpu.with_memory_space_constraint(one, pltpu.VMEM) for one in made])
    return values, token_grad, jnp.swapaxes(grad_a, 0, 1)[None], grad_b[None]


def solution(mesh, nx=4):
    dp, nz = mesh.shape["dp"], mesh.shape["tensor"]
    return jax.shard_map(
        functools.partial(shards, nx, dp // (2 * nx), nz),
        mesh=mesh,
        in_specs=(
            P("dp", "tensor"),
            P("tensor", None),
            P("dp", "tensor", None),
            P("dp", None, "tensor"),
            P("dp", "tensor"),
            P("dp", None),
            P("dp", None),
            P(),
        ),
        out_specs=(
            P("dp", "tensor"),
            P("dp", "tensor"),
            P("dp", "tensor", None),
            P("dp", None, "tensor"),
        ),
        check_vma=False,
    )
```
